32 devices in a mesh: groups: 2 (over y), ctx: 4 (over z), head: 4 (over x, core).
Axes of the slice: x: 2, y: 2, z: 4, core: 2. Of those that a mesh axis runs over, the one named last changes fastest.
Arguments:
- queries: bfloat16 [2048, 4096], P(('groups', 'ctx'), 'head'), parts along dimension 0, may hold values from -250 to 250
- rotated_key_rows: bfloat16 [2048, 1024], P(('groups', 'ctx'), 'head'), parts along dimension 0, may hold values from -6 to 6
- value_state_rows: bfloat16 [2048, 1024], P(('groups', 'ctx'), 'head'), parts along dimension 0, may hold values from -6 to 6
- retained_positions: int32 [8, 32], P(('groups', 'ctx')), parts along dimension 0, may hold values from 0 to 255, as said below
- anchor_length: int32 [2], P('groups'), parts along dimension 0, may hold values from 1 to 128
- out_proj: bfloat16 [4096, 4096], P('head'), may hold values from -0.125 to 0.125
Outputs:
- attn_out: bfloat16 [2048, 4096], P(('groups', 'ctx'), 'head'), parts along dimension 0
The draws below stay inside these ranges and needn't reach their ends.
There are 2 independent parts, one for each index of `groups`. The reference program is written for one: setup_inputs(seed, part) draws one part's arguments, and reference() takes and returns one part's arrays. A program takes and returns all parts, laid end to end along the dimension named above; an argument that names none is the same for every part. Nothing has to cross between parts.
Inputs may be any that keep to these rules, and one draw needn't show every extreme that they name: `retained_positions`: each row holds 32 different positions in increasing order.
All inputs are finite; a program needn't handle non-finite values.
Results may differ from the reference program's by a relative error of at most 0.015.
Values may be sent and summed in bfloat16 or wider, within the bound.
A program may use at most 64 MiB of HBM per device.

```python
import jax
import jax.numpy as jnp
from jax import lax

D = 4096
QUERY_HEADS = 32
KEY_VALUE_HEADS = 8
HEAD_SIZE = 128
BLOCK_TOKENS = 256
ANCHOR = 128
RETAINED_COUNT = 32
DOCUMENT_TOKENS = 1024
N_CTX = 4
N_HEAD = 4


def draw_queries(key, part):
    noise_key = jax.random.fold_in(jax.random.fold_in(key, 11), 0)
    sample = jax.random.normal(noise_key, (DOCUMENT_TOKENS, QUERY_HEADS * HEAD_SIZE), jnp.float32)
    return jnp.clip(sample, -6.0, 6.0).astype(jnp.bfloat16)


def draw_retained_positions(key, part):
    row_keys = jax.random.split(jax.random.fold_in(key, 23), N_CTX)
    orders = jax.vmap(lambda row_key: jax.random.permutation(row_key, BLOCK_TOKENS))(row_keys)
    return jnp.sort(orders[:, :RETAINED_COUNT].astype(jnp.int32), axis=1)


def with_spikes(entries, own_key, source, target, parts, factor):
    owner, partner = [(jnp.arange(entries.shape[dim]) // (entries.shape[dim] // parts)).reshape([-1 if axis == dim else 1 for axis in range(entries.ndim)]) for dim in (source, target)]
    chosen = jax.random.permutation(own_key, parts)[partner]
    strong = (owner == chosen) | (owner == (partner + parts // 2) % parts)
    return jnp.where(strong, factor * entries, entries)


def block_levels(own_key, shape, cuts, smallest, top_value):
    factor_of = 1.0
    for dim, blocks in cuts:
        steps = jax.random.uniform(jax.random.fold_in(jax.random.fold_in(own_key, 6), dim), (blocks,), jnp.float32, smallest / len(cuts), top_value / len(cuts))
        factor_of = factor_of * jnp.repeat(jnp.exp(steps), shape[dim] // blocks).reshape((-1,) + (1,) * (len(shape) - 1 - dim))
    return factor_of


def gaussian(rng, extent, spread, reach, cuts=(), kind=jnp.bfloat16):
    values = spread * jax.random.normal(rng, extent, jnp.float32)
    if cuts:
        values = values * block_levels(rng, extent, cuts, -0.22, 0.18)
    return jnp.clip(values, -reach, reach).astype(kind)


def gaussian_with(own_key, extent, spread, reach, cuts, heavy, kind=jnp.bfloat16):
    array = spread * jax.random.normal(own_key, extent, jnp.float32)
    if cuts:
        array = array * block_levels(own_key, extent, cuts, -0.22, 0.18)
    return jnp.clip(with_spikes(array, jax.random.fold_in(own_key, 3), *heavy), -reach, reach).astype(kind)


def setup_inputs(seed: int = 0, part: int = 0) -> dict:
    streams_of = jax.random.split(jax.random.key(seed), 7)
    part_keys = jax.random.split(jax.random.fold_in(streams_of[6], part), 7)
    return {
        "queries": draw_queries(jax.random.fold_in(jax.random.fold_in(streams_of[6], part), 71), part),
        "rotated_key_rows": gaussian(part_keys[1], (DOCUMENT_TOKENS, KEY_VALUE_HEADS * HEAD_SIZE), 1.0, 6.0, ((0, 4), (1, 4))),
        "value_state_rows": gaussian(part_keys[2], (DOCUMENT_TOKENS, KEY_VALUE_HEADS * HEAD_SIZE), 1.0, 6.0, ((0, 4), (1, 4))),
        "retained_positions": draw_retained_positions(jax.random.fold_in(jax.random.fold_in(streams_of[6], part), 71), part),
        "anchor_length": jax.random.randint(part_keys[4], (1,), 1, ANCHOR + 1).astype(jnp.int32),
        "out_proj": gaussian_with(streams_of[5], (QUERY_HEADS * HEAD_SIZE, D), (QUERY_HEADS * HEAD_SIZE) ** -0.5, 0.125, ((0, 4),), (0, 1, 4, 2.0)),
    }


def reference(queries, rotated_key_rows, value_state_rows, retained_positions, anchor_length, out_proj):
    queries_per_key_head = QUERY_HEADS // KEY_VALUE_HEADS
    inv_root = HEAD_SIZE ** -0.5
    query_head_rows = queries.reshape(N_CTX, BLOCK_TOKENS, KEY_VALUE_HEADS, queries_per_key_head, HEAD_SIZE)
    key_head_rows = rotated_key_rows.reshape(N_CTX, BLOCK_TOKENS, KEY_VALUE_HEADS, HEAD_SIZE)
    value_head_rows = value_state_rows.reshape(N_CTX, BLOCK_TOKENS, KEY_VALUE_HEADS, HEAD_SIZE)
    block_indices = jnp.arange(N_CTX, dtype=jnp.int32)[:, None]
    passing_key_rows = key_head_rows[block_indices, retained_positions].reshape(N_CTX * RETAINED_COUNT, KEY_VALUE_HEADS, HEAD_SIZE)
    passing_value_rows = value_head_rows[block_indices, retained_positions].reshape(N_CTX * RETAINED_COUNT, KEY_VALUE_HEADS, HEAD_SIZE)
    anchor_keys = key_head_rows[0, :ANCHOR]
    anchor_vals = value_head_rows[0, :ANCHOR]
    places = jnp.arange(BLOCK_TOKENS, dtype=jnp.int32)

    def one_host(host_id):
        all_keys = jnp.concatenate([anchor_keys, passing_key_rows, key_head_rows[host_id]], axis=0)
        all_vals = jnp.concatenate([anchor_vals, passing_value_rows, value_head_rows[host_id]], axis=0)
        anchor_ok = (jnp.arange(ANCHOR, dtype=jnp.int32) < anchor_length[0]) & (host_id > 0)
        passed_ok = jnp.arange(N_CTX * RETAINED_COUNT, dtype=jnp.int32) // RETAINED_COUNT < host_id
        allowed = jnp.concatenate([
            jnp.broadcast_to(anchor_ok[None, :], (BLOCK_TOKENS, ANCHOR)),
            jnp.broadcast_to(passed_ok[None, :], (BLOCK_TOKENS, N_CTX * RETAINED_COUNT)),
            places[None, :] <= places[:, None]], axis=1)
        scores = jnp.einsum("tkgd,nkd->kgtn", query_head_rows[host_id].astype(jnp.float32),
                            all_keys.astype(jnp.float32), precision=lax.Precision.HIGHEST) * inv_root
        scores = jnp.where(allowed, scores, -1e30)
        maxima = jnp.max(scores, axis=-1, keepdims=True)
        weights = jnp.where(allowed, jnp.exp(scores - maxima), 0.0)
        totals = jnp.sum(weights, axis=-1)
        rounded = lax.optimization_barrier(weights.astype(jnp.bfloat16)).astype(jnp.float32)
        numerator = jnp.einsum("kgtn,nkd->kgtd", rounded, all_vals.astype(jnp.float32),
                               precision=lax.Precision.HIGHEST)
        result = numerator / totals[..., None]
        return result.transpose(2, 0, 1, 3).reshape(BLOCK_TOKENS, QUERY_HEADS * HEAD_SIZE).astype(jnp.bfloat16)

    attended = lax.map(one_host, jnp.arange(N_CTX, dtype=jnp.int32)).reshape(DOCUMENT_TOKENS, QUERY_HEADS * HEAD_SIZE)
    slab_width = QUERY_HEADS * HEAD_SIZE // N_HEAD
    head_outs = attended.reshape(DOCUMENT_TOKENS, N_HEAD, slab_width).transpose(1, 0, 2)
    head_weights = out_proj.reshape(N_HEAD, slab_width, D)

    def accumulate(running, pieces):
        partial_value = jnp.dot(pieces[0], pieces[1], preferred_element_type=jnp.float32)
        partial_value = lax.optimization_barrier(partial_value.astype(jnp.bfloat16)).astype(jnp.float32)
        return running + partial_value, None

    summed, unused = lax.scan(accumulate, jnp.zeros((DOCUMENT_TOKENS, D), jnp.float32), (head_outs, head_weights))
    return summed.astype(jnp.bfloat16)
```

```python
import functools
import math

import jax
import jax.numpy as jnp
from jax import lax
from jax.experimental import pallas as pl
from jax.experimental.pallas import tpu as pltpu
from jax.sharding import PartitionSpec as P

HEAD_SIZE = 128
ANCHOR = 128
MESH = pl.DeviceIdType.MESH
NEG = -1e30
LAG = 3


def flip(index, mask):
    bit = 1
    while bit <= mask:
        if mask & bit:
            index = index + bit * (1 - 2 * ((index // bit) % 2))
        bit *= 2
    return index


def low_bit(r):
    return r & -r


def dot(a, b, dims=((1,), (0,))):
    return lax.dot_general(a, b, (dims, ((), ())), preferred_element_type=jnp.float32)


def kernel(
    n_ctx, n_head, pos_ref, len_ref, q_hbm, k_hbm, v_hbm, w_hbm, o_ref,
    q_v, kv_v, rem, w_v, acc_s, max_s, sum_s, att, part, outgoing, incoming,
    load_sem, w_sem, pass_send, pass_recv, anc_send, anc_recv, red_send, red_recv,
):
    me_c = lax.axis_index("ctx")
    me_h = lax.axis_index("head")
    tok, q_width = q_v.shape
    kv_width = kv_v.shape[1] // 2
    kv_heads = kv_width // HEAD_SIZE
    per_kv = q_width // kv_width
    retained = pos_ref.shape[1]
    rem_rows = rem.shape[0]
    chunks, _, chunk = part.shape[1:]
    slab = chunks * chunk
    half = tok // 2

    loads = [
        pltpu.make_async_copy(k_hbm, kv_v.at[:, pl.ds(0, kv_width)], load_sem.at[0]),
        pltpu.make_async_copy(v_hbm, kv_v.at[:, pl.ds(kv_width, kv_width)], load_sem.at[1]),
        pltpu.make_async_copy(q_hbm, q_v, load_sem.at[2]),
    ]
    for copy in loads:
        copy.start()

    rem[...] = jnp.zeros_like(rem)

    barrier = pltpu.get_barrier_semaphore()
    for j in range(n_ctx):
        @pl.when(me_c != j)
        def _():
            pl.semaphore_signal(barrier, inc=1, device_id={"ctx": j}, device_id_type=MESH)
    bit, steps = 1, 0
    while bit < n_head:
        pl.semaphore_signal(barrier, inc=1, device_id={"head": flip(me_h, bit)}, device_id_type=MESH)
        bit, steps = 2 * bit, steps + 1

    w_loads = {}
    for r in reversed(range(n_head)):
        columns = pl.ds(pl.multiple_of(flip(me_h, r) * slab, slab), slab)
        w_loads[r] = pltpu.make_async_copy(w_hbm.at[:, columns], w_v.at[r], w_sem.at[r])
        w_loads[r].start()

    loads[0].wait()
    loads[1].wait()
    picked = lax.broadcasted_iota(jnp.int32, (tok, retained), 0) == pos_ref[...]
    kept = dot(picked.astype(jnp.bfloat16), kv_v[...], ((0,), (0,)))
    mine = pl.ds(pl.multiple_of(ANCHOR + me_c * retained, retained), retained)
    rem[mine, :] = kept.astype(jnp.bfloat16)

    pl.semaphore_wait(barrier, n_ctx - 1 + steps)

    def pass_copy(source, target):
        rows = pl.ds(pl.multiple_of(ANCHOR + source * retained, retained), retained)
        return pltpu.make_async_remote_copy(
            src_ref=rem.at[rows, :], dst_ref=rem.at[rows, :],
            send_sem=pass_send.at[target], recv_sem=pass_recv.at[source],
            device_id={"ctx": target}, device_id_type=MESH,
        )

    def anchor_copy(target):
        return pltpu.make_async_remote_copy(
            src_ref=kv_v.at[pl.ds(0, ANCHOR), :], dst_ref=rem.at[pl.ds(0, ANCHOR), :],
            send_sem=anc_send.at[target], recv_sem=anc_recv,
            device_id={"ctx": target}, device_id_type=MESH,
        )

    for j in reversed(range(1, n_ctx)):
        @pl.when(me_c == 0)
        def _():
            anchor_copy(j).start()
    for j in reversed(range(1, n_ctx)):
        @pl.when(me_c < j)
        def _():
            pass_copy(me_c, j).start()

    scale = HEAD_SIZE ** -0.5 * math.log2(math.e)
    loads[2].wait()

    causal = jnp.where(
        lax.broadcasted_iota(jnp.int32, (half, half), 1)
        <= lax.broadcasted_iota(jnp.int32, (half, half), 0),
        0.0, NEG,
    )
    for h in range(kv_heads * per_kv):
        lanes = slice(h * HEAD_SIZE, (h + 1) * HEAD_SIZE)
        k = h // per_kv
        key_lanes = slice(k * HEAD_SIZE, (k + 1) * HEAD_SIZE)
        val_lanes = slice(kv_width + k * HEAD_SIZE, kv_width + (k + 1) * HEAD_SIZE)
        for top in (0, 1):
            rows = slice(top * half, (top + 1) * half)
            query = q_v[rows, lanes]
            s = dot(query, kv_v[rows, key_lanes], ((1,), (1,))) * scale + causal
            best = jnp.max(s, axis=1, keepdims=True)
            if top:
                s0 = dot(query, kv_v[0:half, key_lanes], ((1,), (1,))) * scale
                best = jnp.maximum(best, jnp.max(s0, axis=1, keepdims=True))
            p = jnp.exp2(s - best)
            total = jnp.sum(p, axis=1, keepdims=True)
            value = dot(p.astype(jnp.bfloat16), kv_v[rows, val_lanes])
            if top:
                p0 = jnp.exp2(s0 - best)
                total = total + jnp.sum(p0, axis=1, keepdims=True)
                value = value + dot(p0.astype(jnp.bfloat16), kv_v[0:half, val_lanes])
            acc_s[rows, lanes] = value
            max_s[h, rows, :] = best
            sum_s[h, rows, :] = total

    for j in range(n_ctx - 1):
        @pl.when(me_c > j)
        def _():
            pass_copy(j, me_c).wait_recv()

    @pl.when(me_c > 0)
    def _():
        anchor_copy(me_c).wait_recv()

    place = lax.broadcasted_iota(jnp.int32, (1, rem_rows), 1)
    seen_anchor = (place < jnp.minimum(len_ref[0], ANCHOR)) & (me_c > 0)
    seen_pass = (place >= ANCHOR) & (place - ANCHOR < me_c * retained)
    bias = jnp.where(seen_anchor | seen_pass, 0.0, NEG)
    for h in range(kv_heads * per_kv):
        lanes = slice(h * HEAD_SIZE, (h + 1) * HEAD_SIZE)
        k = h // per_kv
        key_lanes = slice(k * HEAD_SIZE, (k + 1) * HEAD_SIZE)
        val_lanes = slice(kv_width + k * HEAD_SIZE, kv_width + (k + 1) * HEAD_SIZE)
        for top in (0, 1):
            rows = slice(top * half, (top + 1) * half)
            s = dot(q_v[rows, lanes], rem[:, key_lanes], ((1,), (1,))) * scale + bias
            before = max_s[h, rows, :]
            best = jnp.maximum(before, jnp.max(s, axis=1, keepdims=True))
            p = jnp.exp2(s - best)
            fade = jnp.exp2(before - best)
            total = sum_s[h, rows, :] * fade + jnp.sum(p, axis=1, keepdims=True)
            value = acc_s[rows, lanes] * fade + dot(p.astype(jnp.bfloat16), rem[:, val_lanes])
            att[rows, lanes] = (value / total).astype(jnp.bfloat16)

    def red_copy(r, c):
        return pltpu.make_async_remote_copy(
            src_ref=outgoing.at[r - 1, c], dst_ref=incoming.at[r - 1, c],
            send_sem=red_send.at[r - 1, c], recv_sem=red_recv.at[r - 1, c],
            device_id={"head": flip(me_h, low_bit(r))}, device_id_type=MESH,
        )

    def finish(r, c):
        total = part[r, c]
        bit = 1
        while bit < (low_bit(r) if r else n_head):
            red_copy(r + bit, c).wait_recv()
            total = total + incoming[r + bit - 1, c].astype(jnp.float32)
            bit *= 2
        if r:
            outgoing[r - 1, c] = total.astype(jnp.bfloat16)
            red_copy(r, c).start()
        else:
            o_ref[:, c * chunk:(c + 1) * chunk] = total.astype(jnp.bfloat16)

    middle = n_head // 2
    units = [(r, c) for c in range(chunks) for r in reversed(range(middle, n_head))]
    units += [(r, c) for c in range(chunks) for r in reversed(range(middle))]
    late = []
    loaded = set()
    for r, c in units:
        if r not in loaded:
            w_loads[r].wait()
            loaded.add(r)
        value = dot(att[...], w_v[r, :, c * chunk:(c + 1) * chunk])
        if r % 2:
            outgoing[r - 1, c] = value.astype(jnp.bfloat16)
            red_copy(r, c).start()
        else:
            part[r, c] = value
            late.append((r, c))
        while late and (len(late) > LAG or (r < middle and late[0][0] >= middle)):
            finish(*late.pop(0))
    for r, c in late:
        finish(r, c)

    for r, c in units:
        if r:
            red_copy(r, c).wait_send()
    for j in range(1, n_ctx):
        @pl.when(me_c < j)
        def _():
            pass_copy(me_c, j).wait_send()

        @pl.when(me_c == 0)
        def _():
            anchor_copy(j).wait_send()


def local(n_ctx, n_head, queries, rotated_key_rows, value_state_rows, retained_positions, anchor_length, out_proj):
    tok, q_width = queries.shape
    kv_width = rotated_key_rows.shape[1]
    heads = q_width // HEAD_SIZE
    retained = retained_positions.shape[1]
    rem_rows = ANCHOR + n_ctx * retained
    slab = out_proj.shape[1] // n_head
    chunk = math.gcd(slab, 256)
    chunks = slab // chunk
    dma = pltpu.SemaphoreType.DMA
    anywhere = pl.BlockSpec(memory_space=pl.ANY)
    return pl.pallas_call(
        functools.partial(kernel, n_ctx, n_head),
        out_shape=jax.ShapeDtypeStruct((tok, slab), jnp.bfloat16),
        in_specs=[
            pl.BlockSpec(memory_space=pltpu.VMEM),
            pl.BlockSpec(memory_space=pltpu.SMEM),
            anywhere, anywhere, anywhere, anywhere,
        ],
        out_specs=pl.BlockSpec(memory_space=pltpu.VMEM),
        scratch_shapes=[
            pltpu.VMEM((tok, q_width), jnp.bfloat16),
            pltpu.VMEM((tok, 2 * kv_width), jnp.bfloat16),
            pltpu.VMEM((rem_rows, 2 * kv_width), jnp.bfloat16),
            pltpu.VMEM((n_head, q_width, slab), jnp.bfloat16),
            pltpu.VMEM((tok, q_width), jnp.float32),
            pltpu.VMEM((heads, tok, 1), jnp.float32),
            pltpu.VMEM((heads, tok, 1), jnp.float32),
            pltpu.VMEM((tok, q_width), jnp.bfloat16),
            pltpu.VMEM((n_head, chunks, tok, chunk), jnp.float32),
            pltpu.VMEM((n_head - 1, chunks, tok, chunk), jnp.bfloat16),
            pltpu.VMEM((n_head - 1, chunks, tok, chunk), jnp.bfloat16),
            dma((3,)),
            dma((n_head,)),
            dma((n_ctx,)),
            dma((n_ctx,)),
            dma((n_ctx,)),
            dma,
            dma((n_head - 1, chunks)),
            dma((n_head - 1, chunks)),
        ],
        compiler_params=pltpu.CompilerParams(
            collective_id=0, has_side_effects=True, vmem_limit_bytes=48 * 1024 * 1024
        ),
    )(retained_positions, anchor_length, queries, rotated_key_rows, value_state_rows, out_proj)


def solution(mesh):
    placed = (
        P(("groups", "ctx"), "head"),
        P(("groups", "ctx"), "head"),
        P(("groups", "ctx"), "head"),
        P(("groups", "ctx"), None),
        P("groups"),
        P("head", None),
    )
    return jax.shard_map(
        functools.partial(local, mesh.shape["ctx"], mesh.shape["head"]),
        mesh=mesh, in_specs=placed, out_specs=P(("groups", "ctx"), "head"), check_vma=False,
    )
```

```python
import functools
import math

import jax
import jax.numpy as jnp
from jax import lax
from jax.experimental import pallas as pl
from jax.experimental.pallas import tpu as pltpu
from jax.sharding import PartitionSpec as P

HEAD_SIZE = 128
ANCHOR = 128
MESH = pl.DeviceIdType.MESH
NEG = -1e30
LAG = 1
PIECES = 4


def flip(index, mask):
    bit = 1
    while bit <= mask:
        if mask & bit:
            index = index + bit * (1 - 2 * ((index // bit) % 2))
        bit *= 2
    return index


def low_bit(r):
    return r & -r


def dot(a, b, dims=((1,), (0,))):
    return lax.dot_general(a, b, (dims, ((), ())), preferred_element_type=jnp.float32)


def kernel(
    n_ctx, n_head, len_ref, pos_hbm, q_hbm, k_hbm, v_hbm, w_hbm, o_ref,
    pos_v, q_v, kv_v, rem, w_v, acc_s, max_s, sum_s, att, part, outgoing, incoming,
    load_sem, w_sem, pass_send, pass_recv, anc_send, anc_recv, red_send, red_recv,
):
    me_c = lax.axis_index("ctx")
    me_h = lax.axis_index("head")
    tok, q_width = q_v.shape
    kv_width = kv_v.shape[1] // 2
    kv_heads = kv_width // HEAD_SIZE
    per_kv = q_width // kv_width
    retained = pos_v.shape[1]
    rem_rows = rem.shape[0]
    chunks, _, chunk = part.shape
    slab = chunks * chunk
    half = tok // 2
    pieces = anc_recv.shape[0]
    piece = ANCHOR // pieces

    loads = [
        pltpu.make_async_copy(k_hbm, kv_v.at[:, pl.ds(0, kv_width)], load_sem.at[0]),
        pltpu.make_async_copy(v_hbm, kv_v.at[:, pl.ds(kv_width, kv_width)], load_sem.at[1]),
        pltpu.make_async_copy(pos_hbm, pos_v, load_sem.at[2]),
        pltpu.make_async_copy(q_hbm, q_v, load_sem.at[3]),
    ]
    for copy in loads:
        copy.start()

    rem[...] = jnp.zeros_like(rem)

    barrier = pltpu.get_barrier_semaphore()
    for j in range(n_ctx):
        @pl.when(me_c != j)
        def _():
            pl.semaphore_signal(barrier, inc=1, device_id={"ctx": j}, device_id_type=MESH)
    bit, steps = 1, 0
    while bit < n_head:
        pl.semaphore_signal(barrier, inc=1, device_id={"head": flip(me_h, bit)}, device_id_type=MESH)
        bit, steps = 2 * bit, steps + 1

    w_loads = {}
    for r in reversed(range(n_head)):
        columns = pl.ds(pl.multiple_of(flip(me_h, r) * slab, slab), slab)
        w_loads[r] = pltpu.make_async_copy(w_hbm.at[:, columns], w_v.at[r], w_sem.at[r])
        w_loads[r].start()

    def pass_copy(source, target):
        rows = pl.ds(pl.multiple_of(ANCHOR + source * retained, retained), retained)
        return pltpu.make_async_remote_copy(
            src_ref=rem.at[rows, :], dst_ref=rem.at[rows, :],
            send_sem=pass_send.at[target], recv_sem=pass_recv.at[source],
            device_id={"ctx": target}, device_id_type=MESH,
        )

    def anchor_copy(i, origin):
        rows = pl.ds(i * piece, piece)
        return pltpu.make_async_remote_copy(
            src_ref=(kv_v if origin else rem).at[rows, :], dst_ref=rem.at[rows, :],
            send_sem=anc_send.at[i], recv_sem=anc_recv.at[i],
            device_id={"ctx": lax.rem(me_c + 1, n_ctx)}, device_id_type=MESH,
        )

    for copy in loads[:3]:
        copy.wait()
    pl.semaphore_wait(barrier, n_ctx - 1 + steps)

    if n_ctx > 1:
        @pl.when(me_c == 0)
        def _():
            for i in range(pieces):
                anchor_copy(i, True).start()

    picked = lax.broadcasted_iota(jnp.int32, (tok, retained), 0) == pos_v[...]
    kept = dot(picked.astype(jnp.bfloat16), kv_v[...], ((0,), (0,)))
    mine = pl.ds(pl.multiple_of(ANCHOR + me_c * retained, retained), retained)
    rem[mine, :] = kept.astype(jnp.bfloat16)
    for j in reversed(range(1, n_ctx)):
        @pl.when(me_c < j)
        def _():
            pass_copy(me_c, j).start()

    scale = HEAD_SIZE ** -0.5 * math.log2(math.e)
    loads[3].wait()

    causal = jnp.where(
        lax.broadcasted_iota(jnp.int32, (half, half), 1)
        <= lax.broadcasted_iota(jnp.int32, (half, half), 0),
        0.0, NEG,
    )
    causal = jnp.concatenate([causal] * per_kv, axis=0)

    def stacked(k, top):
        rows = slice(top * half, (top + 1) * half)
        return jnp.concatenate(
            [q_v[rows, h * HEAD_SIZE:(h + 1) * HEAD_SIZE] for h in range(k * per_kv, (k + 1) * per_kv)], axis=0
        )

    local_units = [(k, top) for top in (0, 1) for k in range(kv_heads)]
    for number, (k, top) in enumerate(local_units):
        key_lanes = slice(k * HEAD_SIZE, (k + 1) * HEAD_SIZE)
        val_lanes = slice(kv_width + k * HEAD_SIZE, kv_width + (k + 1) * HEAD_SIZE)
        rows = slice(top * half, (top + 1) * half)
        query = stacked(k, top)
        s = dot(query, kv_v[rows, key_lanes], ((1,), (1,))) * scale + causal
        best = jnp.max(s, axis=1, keepdims=True)
        if top:
            s0 = dot(query, kv_v[0:half, key_lanes], ((1,), (1,))) * scale
            best = jnp.maximum(best, jnp.max(s0, axis=1, keepdims=True))
        p = jnp.exp2(s - best)
        total = jnp.sum(p, axis=1, keepdims=True)
        value = dot(p.astype(jnp.bfloat16), kv_v[rows, val_lanes])
        if top:
            p0 = jnp.exp2(s0 - best)
            total = total + jnp.sum(p0, axis=1, keepdims=True)
            value = value + dot(p0.astype(jnp.bfloat16), kv_v[0:half, val_lanes])
        acc_s[k, top] = value
        max_s[k, top] = best
        sum_s[k, top] = total

        @pl.when((me_c > 0) & (me_c < n_ctx - 1))
        def _():
            for i in range(number * pieces // len(local_units), (number + 1) * pieces // len(local_units)):
                anchor_copy(i, False).wait_recv()
                anchor_copy(i, False).start()

    for j in range(n_ctx - 1):
        @pl.when(me_c > j)
        def _():
            pass_copy(j, me_c).wait_recv()

    if n_ctx > 1:
        @pl.when(me_c == n_ctx - 1)
        def _():
            for i in range(pieces):
                anchor_copy(i, False).wait_recv()

    place = lax.broadcasted_iota(jnp.int32, (1, rem_rows), 1)
    seen_anchor = (place < jnp.minimum(len_ref[0], ANCHOR)) & (me_c > 0)
    seen_pass = (place >= ANCHOR) & (place - ANCHOR < me_c * retained)
    bias = jnp.where(seen_anchor | seen_pass, 0.0, NEG)

    def attend(top):
        rows = slice(top * half, (top + 1) * half)
        for k in range(kv_heads):
            key_lanes = slice(k * HEAD_SIZE, (k + 1) * HEAD_SIZE)
            val_lanes = slice(kv_width + k * HEAD_SIZE, kv_width + (k + 1) * HEAD_SIZE)
            s = dot(stacked(k, top), rem[:, key_lanes], ((1,), (1,))) * scale + bias
            before = max_s[k, top]
            best = jnp.maximum(before, jnp.max(s, axis=1, keepdims=True))
            p = jnp.exp2(s - best)
            fade = jnp.exp2(before - best)
            total = sum_s[k, top] * fade + jnp.sum(p, axis=1, keepdims=True)
            value = acc_s[k, top] * fade + dot(p.astype(jnp.bfloat16), rem[:, val_lanes])
            value = (value / total).astype(jnp.bfloat16)
            for g in range(per_kv):
                h = k * per_kv + g
                att[rows, h * HEAD_SIZE:(h + 1) * HEAD_SIZE] = value[g * half:(g + 1) * half]

    def red_copy(r, c, top):
        rows = pl.ds(top * half, half)
        return pltpu.make_async_remote_copy(
            src_ref=outgoing.at[r - 1, c, rows, :], dst_ref=incoming.at[r - 1, c, rows, :],
            send_sem=red_send.at[r - 1, c, top], recv_sem=red_recv.at[r - 1, c, top],
            device_id={"head": flip(me_h, low_bit(r))}, device_id_type=MESH,
        )

    def product(r, c, rows):
        return dot(att[rows, :], w_v[r, :, c * chunk:(c + 1) * chunk])

    def with_received(total, r, c, top, first, last):
        bit = first
        while bit < last:
            red_copy(r + bit, c, top).wait_recv()
            total = total + incoming[r + bit - 1, c, top * half:(top + 1) * half, :].astype(jnp.float32)
            bit *= 2
        return total

    def send(total, r, c, top):
        outgoing[r - 1, c, top * half:(top + 1) * half, :] = total.astype(jnp.bfloat16)
        red_copy(r, c, top).start()

    middle = n_head // 2
    for r in range(middle, n_head):
        w_loads[r].wait()
    for top in (0, 1):
        rows = slice(top * half, (top + 1) * half)
        attend(top)
        late = []
        for c in range(chunks):
            for r in reversed(range(middle, n_head)):
                value = product(r, c, rows)
                if r % 2:
                    send(value, r, c, top)
                else:
                    late.append((value, r, c))
            while len(late) > LAG:
                value, r, d = late.pop(0)
                send(with_received(value, r, d, top, 1, low_bit(r)), r, d, top)
        for value, r, d in late:
            send(with_received(value, r, d, top, 1, low_bit(r)), r, d, top)

    for r in range(middle):
        w_loads[r].wait()
    for r in reversed(range(1, middle)):
        for c in range(chunks):
            value = product(r, c, slice(0, tok))
            for top in (0, 1):
                send(with_received(value[top * half:(top + 1) * half], r, c, top, 1, low_bit(r)), r, c, top)
    for c in range(chunks):
        part[c] = product(0, c, slice(0, tok))
    for c in range(chunks):
        for top in (0, 1):
            rows = slice(top * half, (top + 1) * half)
            part[c, rows, :] = with_received(part[c, rows, :], 0, c, top, 1, middle)
    for top in (0, 1):
        rows = slice(top * half, (top + 1) * half)
        for c in range(chunks):
            total = with_received(part[c, rows, :], 0, c, top, middle, n_head)
            o_ref[rows, c * chunk:(c + 1) * chunk] = total.astype(jnp.bfloat16)

    for r in range(1, n_head):
        for c in range(chunks):
            for top in (0, 1):
                red_copy(r, c, top).wait_send()
    for j in range(1, n_ctx):
        @pl.when(me_c < j)
        def _():
            pass_copy(me_c, j).wait_send()
    if n_ctx > 1:
        @pl.when(me_c < n_ctx - 1)
        def _():
            for i in range(pieces):
                anchor_copy(i, True).wait_send()


def local(n_ctx, n_head, queries, rotated_key_rows, value_state_rows, retained_positions, anchor_length, out_proj):
    tok, q_width = queries.shape
    kv_width = rotated_key_rows.shape[1]
    retained = retained_positions.shape[1]
    rem_rows = ANCHOR + n_ctx * retained
    slab = out_proj.shape[1] // n_head
    chunk = math.gcd(slab, 256)
    chunks = slab // chunk
    dma = pltpu.SemaphoreType.DMA
    held = pl.BlockSpec(memory_space=pltpu.HBM)
    per_kv = q_width // kv_width
    kv_heads = kv_width // HEAD_SIZE
    stack = per_kv * tok // 2
    return pl.pallas_call(
        functools.partial(kernel, n_ctx, n_head),
        out_shape=jax.ShapeDtypeStruct((tok, slab), jnp.bfloat16),
        in_specs=[pl.BlockSpec(memory_space=pltpu.SMEM), held, held, held, held, held],
        out_specs=pl.BlockSpec(memory_space=pltpu.VMEM),
        scratch_shapes=[
            pltpu.VMEM((1, retained), jnp.int32),
            pltpu.VMEM((tok, q_width), jnp.bfloat16),
            pltpu.VMEM((tok, 2 * kv_width), jnp.bfloat16),
            pltpu.VMEM((rem_rows, 2 * kv_width), jnp.bfloat16),
            pltpu.VMEM((n_head, q_width, slab), jnp.bfloat16),
            pltpu.VMEM((kv_heads, 2, stack, HEAD_SIZE), jnp.float32),
            pltpu.VMEM((kv_heads, 2, stack, 1), jnp.float32),
            pltpu.VMEM((kv_heads, 2, stack, 1), jnp.float32),
            pltpu.VMEM((tok, q_width), jnp.bfloat16),
            pltpu.VMEM((chunks, tok, chunk), jnp.float32),
            pltpu.VMEM((n_head - 1, chunks, tok, chunk), jnp.bfloat16),
            pltpu.VMEM((n_head - 1, chunks, tok, chunk), jnp.bfloat16),
            dma((4,)),
            dma((n_head,)),
            dma((n_ctx,)),
            dma((n_ctx,)),
            dma((PIECES,)),
            dma((PIECES,)),
            dma((n_head - 1, chunks, 2)),
            dma((n_head - 1, chunks, 2)),
        ],
        compiler_params=pltpu.CompilerParams(
            collective_id=0, has_side_effects=True, vmem_limit_bytes=48 * 1024 * 1024
        ),
    )(anchor_length, retained_positions, queries, rotated_key_rows, value_state_rows, out_proj)


def solution(mesh):
    placed = (
        P(("groups", "ctx"), "head"),
        P(("groups", "ctx"), "head"),
        P(("groups", "ctx"), "head"),
        P(("groups", "ctx"), None),
        P("groups"),
        P("head", None),
    )
    return jax.shard_map(
        functools.partial(local, mesh.shape["ctx"], mesh.shape["head"]),
        mesh=mesh, in_specs=placed, out_specs=P(("groups", "ctx"), "head"), check_vma=False,
    )
```

```python
import functools
import math

import jax
import jax.numpy as jnp
from jax import lax
from jax.experimental import pallas as pl
from jax.experimental.pallas import tpu as pltpu
from jax.sharding import PartitionSpec as P

HEAD_SIZE = 128
ANCHOR = 128
MESH = pl.DeviceIdType.MESH
NEG = -1e30
LAG = 1


def flip(index, mask):
    bit = 1
    while bit <= mask:
        if mask & bit:
            index = index + bit * (1 - 2 * ((index // bit) % 2))
        bit *= 2
    return index


def low_bit(r):
    return r & -r


def dot(a, b, dims=((1,), (0,))):
    return lax.dot_general(a, b, (dims, ((), ())), preferred_element_type=jnp.float32)


def kernel(
    n_ctx, n_head, len_ref, pos_hbm, q_hbm, k_hbm, v_hbm, w_hbm, o_ref,
    pos_v, q_v, k_v, v_v, rem_k, rem_v, w_v, acc_s, max_s, p_s, att, part, outgoing, incoming,
    load_sem, w_sem, pass_send, pass_recv, anc_send, anc_recv, red_send, red_recv,
):
    me_c = lax.axis_index("ctx")
    me_h = lax.axis_index("head")
    tok, q_width = q_v.shape
    kv_width = k_v.shape[1]
    kv_heads = kv_width // HEAD_SIZE
    per_kv = q_width // kv_width
    retained = pos_v.shape[1]
    rem_rows = rem_k.shape[0]
    chunks, _, chunk = part.shape
    slab = chunks * chunk
    half = tok // 2
    pieces = 2 * kv_heads

    def key_lanes(k):
        return pl.ds(k * HEAD_SIZE, HEAD_SIZE)

    def val_lanes(k):
        return pl.ds(2 * k * HEAD_SIZE, HEAD_SIZE)

    def val_wide(k):
        return pl.ds(2 * k * HEAD_SIZE, 2 * HEAD_SIZE)

    loads = [pltpu.make_async_copy(k_hbm, k_v, load_sem.at[0])]
    loads += [
        pltpu.make_async_copy(v_hbm.at[:, key_lanes(k)], v_v.at[:, val_lanes(k)], load_sem.at[3 + k])
        for k in range(kv_heads)
    ]
    loads.append(pltpu.make_async_copy(pos_hbm, pos_v, load_sem.at[1]))
    load_q = pltpu.make_async_copy(q_hbm, q_v, load_sem.at[2])
    for copy in loads:
        copy.start()
    load_q.start()

    rem_k[...] = jnp.zeros_like(rem_k)
    for k in range(kv_heads):
        ones = slice((2 * k + 1) * HEAD_SIZE, (2 * k + 2) * HEAD_SIZE)
        v_v[:, ones] = jnp.ones((tok, HEAD_SIZE), jnp.bfloat16)
        rem_v[:, ones] = jnp.ones((rem_rows, HEAD_SIZE), jnp.bfloat16)
        rem_v[:, val_lanes(k)] = jnp.zeros((rem_rows, HEAD_SIZE), jnp.bfloat16)

    barrier = pltpu.get_barrier_semaphore()
    for j in range(n_ctx):
        @pl.when(me_c != j)
        def _():
            pl.semaphore_signal(barrier, inc=1, device_id={"ctx": j}, device_id_type=MESH)
    bit, steps = 1, 0
    while bit < n_head:
        pl.semaphore_signal(barrier, inc=1, device_id={"head": flip(me_h, bit)}, device_id_type=MESH)
        bit, steps = 2 * bit, steps + 1

    w_loads = {}
    for r in reversed(range(n_head)):
        columns = pl.ds(pl.multiple_of(flip(me_h, r) * slab, slab), slab)
        w_loads[r] = pltpu.make_async_copy(w_hbm.at[:, columns], w_v.at[r], w_sem.at[r])
        w_loads[r].start()

    def pass_copies(source, target):
        rows = pl.ds(pl.multiple_of(ANCHOR + source * retained, retained), retained)
        refs = [rem_k.at[rows, :]] + [rem_v.at[rows, val_lanes(k)] for k in range(kv_heads)]
        return [
            pltpu.make_async_remote_copy(
                src_ref=ref, dst_ref=ref,
                send_sem=pass_send.at[target, i], recv_sem=pass_recv.at[source, i],
                device_id={"ctx": target}, device_id_type=MESH,
            )
            for i, ref in enumerate(refs)
        ]

    def anchor_copy(i, origin):
        rows = pl.ds(0, ANCHOR)
        if i < kv_heads:
            source, target, lanes = k_v, rem_k, key_lanes(i)
        else:
            source, target, lanes = v_v, rem_v, val_lanes(i - kv_heads)
        return pltpu.make_async_remote_copy(
            src_ref=(source if origin else target).at[rows, lanes], dst_ref=target.at[rows, lanes],
            send_sem=anc_send.at[i], recv_sem=anc_recv.at[i],
            device_id={"ctx": lax.rem(me_c + 1, n_ctx)}, device_id_type=MESH,
        )

    for copy in loads:
        copy.wait()
    pl.semaphore_wait(barrier, n_ctx - 1 + steps)

    if n_ctx > 1:
        @pl.when(me_c == 0)
        def _():
            for i in range(pieces):
                anchor_copy(i, True).start()

    picked = lax.broadcasted_iota(jnp.int32, (tok, retained), 0) == pos_v[...]
    picked = picked.astype(jnp.bfloat16)
    mine = pl.ds(pl.multiple_of(ANCHOR + me_c * retained, retained), retained)
    rem_k[mine, :] = dot(picked, k_v[...], ((0,), (0,))).astype(jnp.bfloat16)
    for k in range(kv_heads):
        rem_v[mine, val_lanes(k)] = dot(picked, v_v[:, val_lanes(k)], ((0,), (0,))).astype(jnp.bfloat16)
    for j in reversed(range(1, n_ctx)):
        @pl.when(me_c < j)
        def _():
            for copy in pass_copies(me_c, j):
                copy.start()

    scale = HEAD_SIZE ** -0.5 * math.log2(math.e)
    load_q.wait()

    causal = jnp.where(
        lax.broadcasted_iota(jnp.int32, (half, half), 1)
        <= lax.broadcasted_iota(jnp.int32, (half, half), 0),
        0.0, NEG,
    )
    causal = jnp.concatenate([causal] * per_kv, axis=0)

    def stacked(k, top):
        rows = slice(top * half, (top + 1) * half)
        return jnp.concatenate(
            [q_v[rows, h * HEAD_SIZE:(h + 1) * HEAD_SIZE] for h in range(k * per_kv, (k + 1) * per_kv)], axis=0
        )

    units = [(k, top) for top in (0, 1) for k in range(kv_heads)]
    for number, (k, top) in enumerate(units):
        rows = slice(top * half, (top + 1) * half)
        query = stacked(k, top)
        s = dot(query, k_v[rows, key_lanes(k)], ((1,), (1,))) * scale + causal
        best = jnp.max(s, axis=1, keepdims=True)
        if top:
            s0 = dot(query, k_v[0:half, key_lanes(k)], ((1,), (1,))) * scale
            best = jnp.max(jnp.maximum(s, s0), axis=1, keepdims=True)
        value = dot(jnp.exp2(s - best).astype(jnp.bfloat16), v_v[rows, val_wide(k)])
        if top:
            value = value + dot(jnp.exp2(s0 - best).astype(jnp.bfloat16), v_v[0:half, val_wide(k)])
        acc_s[k, top] = value
        max_s[k, top] = jnp.broadcast_to(best, max_s.shape[2:])

        @pl.when((me_c > 0) & (me_c < n_ctx - 1))
        def _():
            for i in range(number * pieces // len(units), (number + 1) * pieces // len(units)):
                anchor_copy(i, False).wait_recv()
                anchor_copy(i, False).start()

    def await_remote(first, last):
        for j in range(n_ctx - 1):
            @pl.when(me_c > j)
            def _():
                for copy in pass_copies(j, me_c)[(1 if first else 0):(1 + kv_heads if first else 1)]:
                    copy.wait_recv()
        if n_ctx > 1:
            @pl.when(me_c == n_ctx - 1)
            def _():
                for i in range(first, last):
                    anchor_copy(i, False).wait_recv()

    await_remote(0, kv_heads)
    place = lax.broadcasted_iota(jnp.int32, (1, rem_rows), 1)
    seen_anchor = (place < jnp.minimum(len_ref[0], ANCHOR)) & (me_c > 0)
    seen_pass = (place >= ANCHOR) & (place - ANCHOR < me_c * retained)
    bias = jnp.where(seen_anchor | seen_pass, 0.0, NEG)
    for k, top in units:
        s = dot(stacked(k, top), rem_k[:, key_lanes(k)], ((1,), (1,))) * scale + bias
        before = max_s[k, top]
        best = jnp.maximum(before, jnp.max(s, axis=1, keepdims=True))
        wide = jnp.concatenate([best] * (rem_rows // HEAD_SIZE), axis=1)
        p_s[k, top] = jnp.exp2(s - wide).astype(jnp.bfloat16)
        fade = jnp.exp2(before - best)
        acc_s[k, top] = acc_s[k, top] * jnp.concatenate([fade, fade], axis=1)
    await_remote(kv_heads, pieces)

    def attend(top):
        rows = slice(top * half, (top + 1) * half)
        for k in range(kv_heads):
            value = acc_s[k, top] + dot(p_s[k, top], rem_v[:, val_wide(k)])
            value = (value[:, :HEAD_SIZE] / value[:, HEAD_SIZE:]).astype(jnp.bfloat16)
            for g in range(per_kv):
                h = k * per_kv + g
                att[rows, h * HEAD_SIZE:(h + 1) * HEAD_SIZE] = value[g * half:(g + 1) * half]

    def red_copy(r, c, top):
        rows = pl.ds(top * half, half)
        return pltpu.make_async_remote_copy(
            src_ref=outgoing.at[r - 1, c, rows, :], dst_ref=incoming.at[r - 1, c, rows, :],
            send_sem=red_send.at[r - 1, c, top], recv_sem=red_recv.at[r - 1, c, top],
            device_id={"head": flip(me_h, low_bit(r))}, device_id_type=MESH,
        )

    def product(r, c, rows):
        return dot(att[rows, :], w_v[r, :, c * chunk:(c + 1) * chunk])

    def with_received(total, r, c, top, first, last):
        bit = first
        while bit < last:
            red_copy(r + bit, c, top).wait_recv()
            total = total + incoming[r + bit - 1, c, top * half:(top + 1) * half, :].astype(jnp.float32)
            bit *= 2
        return total

    def send(total, r, c, top):
        outgoing[r - 1, c, top * half:(top + 1) * half, :] = total.astype(jnp.bfloat16)
        red_copy(r, c, top).start()

    middle = n_head // 2
    for r in range(middle, n_head):
        w_loads[r].wait()
    for top in (0, 1):
        rows = slice(top * half, (top + 1) * half)
        attend(top)
        late = []
        for c in range(chunks):
            for r in reversed(range(middle, n_head)):
                value = product(r, c, rows)
                if r % 2:
                    send(value, r, c, top)
                else:
                    late.append((value, r, c))
            while len(late) > LAG:
                value, r, d = late.pop(0)
                send(with_received(value, r, d, top, 1, low_bit(r)), r, d, top)
        for value, r, d in late:
            send(with_received(value, r, d, top, 1, low_bit(r)), r, d, top)

    for r in range(middle):
        w_loads[r].wait()
    for r in reversed(range(1, middle)):
        for c in range(chunks):
            value = product(r, c, slice(0, tok))
            for top in (0, 1):
                send(with_received(value[top * half:(top + 1) * half], r, c, top, 1, low_bit(r)), r, c, top)
    for c in range(chunks):
        part[c] = product(0, c, slice(0, tok))
    for c in range(chunks):
        for top in (0, 1):
            rows = slice(top * half, (top + 1) * half)
            part[c, rows, :] = with_received(part[c, rows, :], 0, c, top, 1, middle)
    for top in (0, 1):
        rows = slice(top * half, (top + 1) * half)
        for c in range(chunks):
            total = with_received(part[c, rows, :], 0, c, top, middle, n_head)
            o_ref[rows, c * chunk:(c + 1) * chunk] = total.astype(jnp.bfloat16)

    for r in range(1, n_head):
        for c in range(chunks):
            for top in (0, 1):
                red_copy(r, c, top).wait_send()
    for j in range(1, n_ctx):
        @pl.when(me_c < j)
        def _():
            for copy in pass_copies(me_c, j):
                copy.wait_send()
    if n_ctx > 1:
        @pl.when(me_c < n_ctx - 1)
        def _():
            for i in range(pieces):
                anchor_copy(i, True).wait_send()


def local(n_ctx, n_head, queries, rotated_key_rows, value_state_rows, retained_positions, anchor_length, out_proj):
    tok, q_width = queries.shape
    kv_width = rotated_key_rows.shape[1]
    retained = retained_positions.shape[1]
    rem_rows = pl.cdiv(ANCHOR + n_ctx * retained, HEAD_SIZE) * HEAD_SIZE
    slab = out_proj.shape[1] // n_head
    chunk = math.gcd(slab, 256)
    chunks = slab // chunk
    dma = pltpu.SemaphoreType.DMA
    held = pl.BlockSpec(memory_space=pltpu.HBM)
    per_kv = q_width // kv_width
    kv_heads = kv_width // HEAD_SIZE
    stack = per_kv * tok // 2
    operands = [
        pltpu.with_memory_space_constraint(array, pltpu.HBM)
        for array in (retained_positions, queries, rotated_key_rows, value_state_rows, out_proj)
    ]
    return pl.pallas_call(
        functools.partial(kernel, n_ctx, n_head),
        out_shape=jax.ShapeDtypeStruct((tok, slab), jnp.bfloat16),
        in_specs=[pl.BlockSpec(memory_space=pltpu.SMEM), held, held, held, held, held],
        out_specs=pl.BlockSpec(memory_space=pltpu.VMEM),
        scratch_shapes=[
            pltpu.VMEM((1, retained), jnp.int32),
            pltpu.VMEM((tok, q_width), jnp.bfloat16),
            pltpu.VMEM((tok, kv_width), jnp.bfloat16),
            pltpu.VMEM((tok, 2 * kv_width), jnp.bfloat16),
            pltpu.VMEM((rem_rows, kv_width), jnp.bfloat16),
            pltpu.VMEM((rem_rows, 2 * kv_width), jnp.bfloat16),
            pltpu.VMEM((n_head, q_width, slab), jnp.bfloat16),
            pltpu.VMEM((kv_heads, 2, stack, 2 * HEAD_SIZE), jnp.float32),
            pltpu.VMEM((kv_heads, 2, stack, HEAD_SIZE), jnp.float32),
            pltpu.VMEM((kv_heads, 2, stack, rem_rows), jnp.bfloat16),
            pltpu.VMEM((tok, q_width), jnp.bfloat16),
            pltpu.VMEM((chunks, tok, chunk), jnp.float32),
            pltpu.VMEM((n_head - 1, chunks, tok, chunk), jnp.bfloat16),
            pltpu.VMEM((n_head - 1, chunks, tok, chunk), jnp.bfloat16),
            dma((3 + kv_heads,)),
            dma((n_head,)),
            dma((n_ctx, 1 + kv_heads)),
            dma((n_ctx, 1 + kv_heads)),
            dma((2 * kv_heads,)),
            dma((2 * kv_heads,)),
            dma((n_head - 1, chunks, 2)),
            dma((n_head - 1, chunks, 2)),
        ],
        compiler_params=pltpu.CompilerParams(
            collective_id=0, has_side_effects=True, vmem_limit_bytes=48 * 1024 * 1024
        ),
    )(anchor_length, *operands)


def solution(mesh):
    placed = (
        P(("groups", "ctx"), "head"),
        P(("groups", "ctx"), "head"),
        P(("groups", "ctx"), "head"),
        P(("groups", "ctx"), None),
        P("groups"),
        P("head", None),
    )
    return jax.shard_map(
        functools.partial(local, mesh.shape["ctx"], mesh.shape["head"]),
        mesh=mesh, in_specs=placed, out_specs=P(("groups", "ctx"), "head"), check_vma=False,
    )
```

```python
import functools
import math

import jax
import jax.numpy as jnp
from jax import lax
from jax.experimental import pallas as pl
from jax.experimental.pallas import tpu as pltpu
from jax.sharding import PartitionSpec as P

HEAD_SIZE = 128
ANCHOR = 128
MESH = pl.DeviceIdType.MESH
NEG = -1e30
LAG = 1


def flip(index, mask):
    bit = 1
    while bit <= mask:
        if mask & bit:
            index = index + bit * (1 - 2 * ((index // bit) % 2))
        bit *= 2
    return index


def low_bit(r):
    return r & -r


def dot(a, b, dims=((1,), (0,))):
    return lax.dot_general(a, b, (dims, ((), ())), preferred_element_type=jnp.float32)


def kernel(
    n_ctx, n_head, len_ref, pos_hbm, q_hbm, k_hbm, v_hbm, w_hbm, o_ref,
    pos_v, q_v, k_v, v_v, rem_k, rem_v, w_v, acc_s, max_s, p_s, att, part, outgoing, incoming,
    load_sem, w_sem, pass_send, pass_recv, anc_send, anc_recv, red_send, red_recv,
):
    me_c = lax.axis_index("ctx")
    me_h = lax.axis_index("head")
    tok, q_width = q_v.shape
    kv_width = k_v.shape[1]
    kv_heads = kv_width // HEAD_SIZE
    per_kv = q_width // kv_width
    retained = pos_v.shape[1]
    rem_rows = rem_k.shape[0]
    chunks, _, chunk = part.shape
    slab = chunks * chunk
    half = tok // 2
    pieces = 2 * kv_heads

    def key_lanes(k):
        return pl.ds(k * HEAD_SIZE, HEAD_SIZE)

    def val_lanes(k):
        return pl.ds(2 * k * HEAD_SIZE, HEAD_SIZE)

    def val_wide(k):
        return pl.ds(2 * k * HEAD_SIZE, 2 * HEAD_SIZE)

    loads = [pltpu.make_async_copy(k_hbm, k_v, load_sem.at[0])]
    loads += [
        pltpu.make_async_copy(v_hbm.at[:, key_lanes(k)], v_v.at[:, val_lanes(k)], load_sem.at[3 + k])
        for k in range(kv_heads)
    ]
    loads.append(pltpu.make_async_copy(pos_hbm, pos_v, load_sem.at[1]))
    load_q = pltpu.make_async_copy(q_hbm, q_v, load_sem.at[2])
    for copy in loads:
        copy.start()
    load_q.start()

    rem_k[...] = jnp.zeros_like(rem_k)
    for k in range(kv_heads):
        ones = slice((2 * k + 1) * HEAD_SIZE, (2 * k + 2) * HEAD_SIZE)
        v_v[:, ones] = jnp.ones((tok, HEAD_SIZE), jnp.bfloat16)
        rem_v[:, ones] = jnp.ones((rem_rows, HEAD_SIZE), jnp.bfloat16)
        rem_v[:, val_lanes(k)] = jnp.zeros((rem_rows, HEAD_SIZE), jnp.bfloat16)

    barrier = pltpu.get_barrier_semaphore()
    @pl.when(me_c > 0)
    def _():
        before = lax.rem(me_c + n_ctx - 1, n_ctx)
        pl.semaphore_signal(barrier, inc=1, device_id={"ctx": before}, device_id_type=MESH)
    bit, steps = 1, 0
    while bit < n_head:
        pl.semaphore_signal(barrier, inc=1, device_id={"head": flip(me_h, bit)}, device_id_type=MESH)
        bit, steps = 2 * bit, steps + 1

    w_loads = {}
    for r in reversed(range(n_head)):
        columns = pl.ds(pl.multiple_of(flip(me_h, r) * slab, slab), slab)
        w_loads[r] = pltpu.make_async_copy(w_hbm.at[:, columns], w_v.at[r], w_sem.at[r])
        w_loads[r].start()

    def pass_copies(source):
        rows = pl.ds(pl.multiple_of(ANCHOR + source * retained, retained), retained)
        refs = [rem_k.at[rows, :]] + [rem_v.at[rows, val_lanes(k)] for k in range(kv_heads)]
        return [
            pltpu.make_async_remote_copy(
                src_ref=ref, dst_ref=ref,
                send_sem=pass_send.at[source, i], recv_sem=pass_recv.at[source, i],
                device_id={"ctx": lax.rem(me_c + 1, n_ctx)}, device_id_type=MESH,
            )
            for i, ref in enumerate(refs)
        ]

    def anchor_copy(i, origin):
        rows = pl.ds(0, ANCHOR)
        if i < kv_heads:
            source, target, lanes = k_v, rem_k, key_lanes(i)
        else:
            source, target, lanes = v_v, rem_v, val_lanes(i - kv_heads)
        return pltpu.make_async_remote_copy(
            src_ref=(source if origin else target).at[rows, lanes], dst_ref=target.at[rows, lanes],
            send_sem=anc_send.at[i], recv_sem=anc_recv.at[i],
            device_id={"ctx": lax.rem(me_c + 1, n_ctx)}, device_id_type=MESH,
        )

    for copy in loads:
        copy.wait()
    @pl.when(me_c < n_ctx - 1)
    def _():
        pl.semaphore_wait(barrier, steps + 1)

    @pl.when(me_c == n_ctx - 1)
    def _():
        pl.semaphore_wait(barrier, steps)

    def start_anchor(first, last):
        if n_ctx > 1:
            @pl.when(me_c == 0)
            def _():
                for i in range(first, last):
                    anchor_copy(i, True).start()

    start_anchor(0, kv_heads)
    picked = lax.broadcasted_iota(jnp.int32, (tok, retained), 0) == pos_v[...]
    picked = picked.astype(jnp.bfloat16)
    mine = pl.ds(pl.multiple_of(ANCHOR + me_c * retained, retained), retained)
    rem_k[mine, :] = dot(picked, k_v[...], ((0,), (0,))).astype(jnp.bfloat16)
    for k in range(kv_heads):
        rem_v[mine, val_lanes(k)] = dot(picked, v_v[:, val_lanes(k)], ((0,), (0,))).astype(jnp.bfloat16)
    @pl.when(me_c < n_ctx - 1)
    def _():
        for copy in pass_copies(me_c):
            copy.start()

    start_anchor(kv_heads, pieces)

    def forward_pass(source):
        @pl.when((me_c > source) & (me_c < n_ctx - 1))
        def _():
            for copy in pass_copies(source):
                copy.wait_recv()
                copy.start()

    scale = HEAD_SIZE ** -0.5 * math.log2(math.e)
    load_q.wait()

    causal = jnp.where(
        lax.broadcasted_iota(jnp.int32, (half, half), 1)
        <= lax.broadcasted_iota(jnp.int32, (half, half), 0),
        0.0, NEG,
    )
    causal = jnp.concatenate([causal] * per_kv, axis=0)

    def stacked(k, top):
        rows = slice(top * half, (top + 1) * half)
        return jnp.concatenate(
            [q_v[rows, h * HEAD_SIZE:(h + 1) * HEAD_SIZE] for h in range(k * per_kv, (k + 1) * per_kv)], axis=0
        )

    units = [(k, top) for top in (0, 1) for k in range(kv_heads)]
    for number, (k, top) in enumerate(units):
        rows = slice(top * half, (top + 1) * half)
        query = stacked(k, top)
        s = dot(query, k_v[rows, key_lanes(k)], ((1,), (1,))) * scale + causal
        best = jnp.max(s, axis=1, keepdims=True)
        if top:
            s0 = dot(query, k_v[0:half, key_lanes(k)], ((1,), (1,))) * scale
            best = jnp.max(jnp.maximum(s, s0), axis=1, keepdims=True)
        value = dot(jnp.exp2(s - best).astype(jnp.bfloat16), v_v[rows, val_wide(k)])
        if top:
            value = value + dot(jnp.exp2(s0 - best).astype(jnp.bfloat16), v_v[0:half, val_wide(k)])
        acc_s[k, top] = value
        max_s[k, top] = jnp.broadcast_to(best, max_s.shape[2:])

        if number == 0:
            for source in reversed(range(1, n_ctx - 1)):
                forward_pass(source)

        @pl.when((me_c > 0) & (me_c < n_ctx - 1))
        def _():
            anchor_copy(number, False).wait_recv()
            anchor_copy(number, False).start()

        if number == kv_heads - 1 and n_ctx > 1:
            forward_pass(0)

    def await_remote(values):
        @pl.when((me_c == n_ctx - 1) & (me_c > 0))
        def _():
            for source in range(n_ctx - 1):
                copies = pass_copies(source)
                for copy in copies[1:] if values else copies[:1]:
                    copy.wait_recv()
            for k in range(kv_heads):
                anchor_copy(k + values * kv_heads, False).wait_recv()

    await_remote(0)
    place = lax.broadcasted_iota(jnp.int32, (1, rem_rows), 1)
    seen_anchor = (place < jnp.minimum(len_ref[0], ANCHOR)) & (me_c > 0)
    seen_pass = (place >= ANCHOR) & (place - ANCHOR < me_c * retained)
    bias = jnp.where(seen_anchor | seen_pass, 0.0, NEG)

    def weigh(top):
        for k in range(kv_heads):
            s = dot(stacked(k, top), rem_k[:, key_lanes(k)], ((1,), (1,))) * scale + bias
            before = max_s[k, top]
            best = jnp.maximum(before, jnp.max(s, axis=1, keepdims=True))
            wide = jnp.concatenate([best] * (rem_rows // HEAD_SIZE), axis=1)
            p_s[k, top] = jnp.exp2(s - wide).astype(jnp.bfloat16)
            fade = jnp.exp2(before - best)
            acc_s[k, top] = acc_s[k, top] * jnp.concatenate([fade, fade], axis=1)

    def attend(top):
        rows = slice(top * half, (top + 1) * half)
        for k in range(kv_heads):
            value = acc_s[k, top] + dot(p_s[k, top], rem_v[:, val_wide(k)])
            value = (value[:, :HEAD_SIZE] / value[:, HEAD_SIZE:]).astype(jnp.bfloat16)
            for g in range(per_kv):
                h = k * per_kv + g
                att[rows, h * HEAD_SIZE:(h + 1) * HEAD_SIZE] = value[g * half:(g + 1) * half]

    def red_copy(r, c, top):
        rows = pl.ds(top * half, half)
        return pltpu.make_async_remote_copy(
            src_ref=outgoing.at[r - 1, c, rows, :], dst_ref=incoming.at[r - 1, c, rows, :],
            send_sem=red_send.at[r - 1, c, top], recv_sem=red_recv.at[r - 1, c, top],
            device_id={"head": flip(me_h, low_bit(r))}, device_id_type=MESH,
        )

    def product(r, c, rows):
        return dot(att[rows, :], w_v[r, :, c * chunk:(c + 1) * chunk])

    def with_received(total, r, c, top, first, last):
        bit = first
        while bit < last:
            red_copy(r + bit, c, top).wait_recv()
            total = total + incoming[r + bit - 1, c, top * half:(top + 1) * half, :].astype(jnp.float32)
            bit *= 2
        return total

    def send(total, r, c, top):
        outgoing[r - 1, c, top * half:(top + 1) * half, :] = total.astype(jnp.bfloat16)
        red_copy(r, c, top).start()

    middle = n_head // 2
    for r in range(middle, n_head):
        w_loads[r].wait()
    for top in (0, 1):
        rows = slice(top * half, (top + 1) * half)
        weigh(top)
        if top == 0:
            await_remote(1)
        attend(top)
        late = []
        for c in range(chunks):
            for r in reversed(range(middle, n_head)):
                value = product(r, c, rows)
                if r % 2:
                    send(value, r, c, top)
                else:
                    late.append((value, r, c))
            while len(late) > LAG:
                value, r, d = late.pop(0)
                send(with_received(value, r, d, top, 1, low_bit(r)), r, d, top)
        for value, r, d in late:
            send(with_received(value, r, d, top, 1, low_bit(r)), r, d, top)

    for r in range(middle):
        w_loads[r].wait()
    for r in reversed(range(1, middle)):
        for c in range(chunks):
            value = product(r, c, slice(0, tok))
            for top in (0, 1):
                send(with_received(value[top * half:(top + 1) * half], r, c, top, 1, low_bit(r)), r, c, top)
    for c in range(chunks):
        part[c] = product(0, c, slice(0, tok))
    for c in range(chunks):
        for top in (0, 1):
            rows = slice(top * half, (top + 1) * half)
            part[c, rows, :] = with_received(part[c, rows, :], 0, c, top, 1, middle)
    for top in (0, 1):
        rows = slice(top * half, (top + 1) * half)
        for c in range(chunks):
            total = with_received(part[c, rows, :], 0, c, top, middle, n_head)
            o_ref[rows, c * chunk:(c + 1) * chunk] = total.astype(jnp.bfloat16)

    for r in range(1, n_head):
        for c in range(chunks):
            for top in (0, 1):
                red_copy(r, c, top).wait_send()
    @pl.when(me_c < n_ctx - 1)
    def _():
        for i in range(pieces):
            anchor_copy(i, True).wait_send()
    for source in range(n_ctx - 1):
        @pl.when((me_c >= source) & (me_c < n_ctx - 1))
        def _():
            for copy in pass_copies(source):
                copy.wait_send()


def local(n_ctx, n_head, queries, rotated_key_rows, value_state_rows, retained_positions, anchor_length, out_proj):
    tok, q_width = queries.shape
    kv_width = rotated_key_rows.shape[1]
    retained = retained_positions.shape[1]
    rem_rows = pl.cdiv(ANCHOR + n_ctx * retained, HEAD_SIZE) * HEAD_SIZE
    slab = out_proj.shape[1] // n_head
    chunk = math.gcd(slab, 256)
    chunks = slab // chunk
    dma = pltpu.SemaphoreType.DMA
    held = pl.BlockSpec(memory_space=pltpu.HBM)
    per_kv = q_width // kv_width
    kv_heads = kv_width // HEAD_SIZE
    stack = per_kv * tok // 2
    operands = [
        pltpu.with_memory_space_constraint(array, pltpu.HBM)
        for array in (retained_positions, queries, rotated_key_rows, value_state_rows, out_proj)
    ]
    return pl.pallas_call(
        functools.partial(kernel, n_ctx, n_head),
        out_shape=jax.ShapeDtypeStruct((tok, slab), jnp.bfloat16),
        in_specs=[pl.BlockSpec(memory_space=pltpu.SMEM), held, held, held, held, held],
        out_specs=pl.BlockSpec(memory_space=pltpu.VMEM),
        scratch_shapes=[
            pltpu.VMEM((1, retained), jnp.int32),
            pltpu.VMEM((tok, q_width), jnp.bfloat16),
            pltpu.VMEM((tok, kv_width), jnp.bfloat16),
            pltpu.VMEM((tok, 2 * kv_width), jnp.bfloat16),
            pltpu.VMEM((rem_rows, kv_width), jnp.bfloat16),
            pltpu.VMEM((rem_rows, 2 * kv_width), jnp.bfloat16),
            pltpu.VMEM((n_head, q_width, slab), jnp.bfloat16),
            pltpu.VMEM((kv_heads, 2, stack, 2 * HEAD_SIZE), jnp.float32),
            pltpu.VMEM((kv_heads, 2, stack, HEAD_SIZE), jnp.float32),
            pltpu.VMEM((kv_heads, 2, stack, rem_rows), jnp.bfloat16),
            pltpu.VMEM((tok, q_width), jnp.bfloat16),
            pltpu.VMEM((chunks, tok, chunk), jnp.float32),
            pltpu.VMEM((n_head - 1, chunks, tok, chunk), jnp.bfloat16),
            pltpu.VMEM((n_head - 1, chunks, tok, chunk), jnp.bfloat16),
            dma((3 + kv_heads,)),
            dma((n_head,)),
            dma((n_ctx, 1 + kv_heads)),
            dma((n_ctx, 1 + kv_heads)),
            dma((2 * kv_heads,)),
            dma((2 * kv_heads,)),
            dma((n_head - 1, chunks, 2)),
            dma((n_head - 1, chunks, 2)),
        ],
        compiler_params=pltpu.CompilerParams(
            collective_id=0, has_side_effects=True, vmem_limit_bytes=48 * 1024 * 1024
        ),
    )(anchor_length, *operands)


def solution(mesh):
    placed = (
        P(("groups", "ctx"), "head"),
        P(("groups", "ctx"), "head"),
        P(("groups", "ctx"), "head"),
        P(("groups", "ctx"), None),
        P("groups"),
        P("head", None),
    )
    return jax.shard_map(
        functools.partial(local, mesh.shape["ctx"], mesh.shape["head"]),
        mesh=mesh, in_specs=placed, out_specs=P(("groups", "ctx"), "head"), check_vma=False,
    )
```

```python
import functools
import math

import jax
import jax.numpy as jnp
from jax import lax
from jax.experimental import pallas as pl
from jax.experimental.pallas import tpu as pltpu
from jax.sharding import PartitionSpec as P

HEAD_SIZE = 128
ANCHOR = 128
MESH = pl.DeviceIdType.MESH
NEG = -1e30
LAG = 1


def flip(index, mask):
    bit = 1
    while bit <= mask:
        if mask & bit:
            index = index + bit * (1 - 2 * ((index // bit) % 2))
        bit *= 2
    return index


def low_bit(r):
    return r & -r


def dot(a, b, dims=((1,), (0,))):
    return lax.dot_general(a, b, (dims, ((), ())), preferred_element_type=jnp.float32)


def kernel(
    n_ctx, n_head, len_ref, pos_hbm, q_hbm, k_hbm, v_hbm, w_hbm, o_ref,
    pos_v, q_v, k_v, v_v, rem_k, rem_v, w_v, acc_s, max_s, p_s, att, part, outgoing, incoming, relay,
    load_sem, w_sem, pass_send, pass_recv, anc_send, anc_recv, red_send, red_recv, relay_send, relay_recv,
):
    me_c = lax.axis_index("ctx")
    me_h = lax.axis_index("head")
    tok, q_width = q_v.shape
    kv_width = k_v.shape[1]
    kv_heads = kv_width // HEAD_SIZE
    per_kv = q_width // kv_width
    retained = pos_v.shape[1]
    rem_rows = rem_k.shape[0]
    chunks, _, chunk = part.shape
    slab = chunks * chunk
    half = tok // 2
    pieces = 2 * kv_heads
    middle = n_head // 2
    pairs = min(2, n_ctx // 2) if n_head > 1 else 0

    def key_lanes(k):
        return pl.ds(k * HEAD_SIZE, HEAD_SIZE)

    def val_lanes(k):
        return pl.ds(2 * k * HEAD_SIZE, HEAD_SIZE)

    def val_wide(k):
        return pl.ds(2 * k * HEAD_SIZE, 2 * HEAD_SIZE)

    loads = [pltpu.make_async_copy(k_hbm, k_v, load_sem.at[0])]
    loads += [
        pltpu.make_async_copy(v_hbm.at[:, key_lanes(k)], v_v.at[:, val_lanes(k)], load_sem.at[3 + k])
        for k in range(kv_heads)
    ]
    loads.append(pltpu.make_async_copy(pos_hbm, pos_v, load_sem.at[1]))
    load_q = pltpu.make_async_copy(q_hbm, q_v, load_sem.at[2])
    for copy in loads:
        copy.start()
    load_q.start()

    rem_k[...] = jnp.zeros_like(rem_k)
    for k in range(kv_heads):
        ones = slice((2 * k + 1) * HEAD_SIZE, (2 * k + 2) * HEAD_SIZE)
        v_v[:, ones] = jnp.ones((tok, HEAD_SIZE), jnp.bfloat16)
        rem_v[:, ones] = jnp.ones((rem_rows, HEAD_SIZE), jnp.bfloat16)
        rem_v[:, val_lanes(k)] = jnp.zeros((rem_rows, HEAD_SIZE), jnp.bfloat16)

    barrier = pltpu.get_barrier_semaphore()
    @pl.when(me_c > 0)
    def _():
        before = lax.rem(me_c + n_ctx - 1, n_ctx)
        pl.semaphore_signal(barrier, inc=1, device_id={"ctx": before}, device_id_type=MESH)
    bit, steps = 1, 0
    while bit < n_head:
        pl.semaphore_signal(barrier, inc=1, device_id={"head": flip(me_h, bit)}, device_id_type=MESH)
        bit, steps = 2 * bit, steps + 1
    for i in range(pairs):
        @pl.when(me_c == i)
        def _():
            pl.semaphore_signal(barrier, inc=1, device_id={"ctx": n_ctx - 1 - i}, device_id_type=MESH)

        @pl.when(me_c == n_ctx - 1 - i)
        def _():
            other = {"ctx": i, "head": flip(me_h, middle)}
            pl.semaphore_signal(barrier, inc=1, device_id=other, device_id_type=MESH)

    w_loads = {}
    for r in reversed(range(n_head)):
        columns = pl.ds(pl.multiple_of(flip(me_h, r) * slab, slab), slab)
        w_loads[r] = pltpu.make_async_copy(w_hbm.at[:, columns], w_v.at[r], w_sem.at[r])
        w_loads[r].start()

    def pass_copies(source):
        rows = pl.ds(pl.multiple_of(ANCHOR + source * retained, retained), retained)
        refs = [rem_k.at[rows, :]] + [rem_v.at[rows, val_lanes(k)] for k in range(kv_heads)]
        return [
            pltpu.make_async_remote_copy(
                src_ref=ref, dst_ref=ref,
                send_sem=pass_send.at[source, i], recv_sem=pass_recv.at[source, i],
                device_id={"ctx": lax.rem(me_c + 1, n_ctx)}, device_id_type=MESH,
            )
            for i, ref in enumerate(refs)
        ]

    def anchor_copy(i, origin):
        rows = pl.ds(0, ANCHOR)
        if i < kv_heads:
            source, target, lanes = k_v, rem_k, key_lanes(i)
        else:
            source, target, lanes = v_v, rem_v, val_lanes(i - kv_heads)
        return pltpu.make_async_remote_copy(
            src_ref=(source if origin else target).at[rows, lanes], dst_ref=target.at[rows, lanes],
            send_sem=anc_send.at[i], recv_sem=anc_recv.at[i],
            device_id={"ctx": lax.rem(me_c + 1, n_ctx)}, device_id_type=MESH,
        )

    for copy in loads:
        copy.wait()
    for j in range(n_ctx):
        greeted = steps + (j < n_ctx - 1) + (j < pairs or j >= n_ctx - pairs)

        @pl.when(me_c == j)
        def _():
            pl.semaphore_wait(barrier, greeted)

    def start_anchor(first, last):
        if n_ctx > 1:
            @pl.when(me_c == 0)
            def _():
                for i in range(first, last):
                    anchor_copy(i, True).start()

    start_anchor(0, kv_heads)
    picked = lax.broadcasted_iota(jnp.int32, (tok, retained), 0) == pos_v[...]
    picked = picked.astype(jnp.bfloat16)
    mine = pl.ds(pl.multiple_of(ANCHOR + me_c * retained, retained), retained)
    rem_k[mine, :] = dot(picked, k_v[...], ((0,), (0,))).astype(jnp.bfloat16)
    for k in range(kv_heads):
        rem_v[mine, val_lanes(k)] = dot(picked, v_v[:, val_lanes(k)], ((0,), (0,))).astype(jnp.bfloat16)
    @pl.when(me_c < n_ctx - 1)
    def _():
        for copy in pass_copies(me_c):
            copy.start()

    start_anchor(kv_heads, pieces)

    def forward_pass(source):
        @pl.when((me_c > source) & (me_c < n_ctx - 1))
        def _():
            for copy in pass_copies(source):
                copy.wait_recv()
                copy.start()

    scale = HEAD_SIZE ** -0.5 * math.log2(math.e)
    load_q.wait()

    causal = jnp.where(
        lax.broadcasted_iota(jnp.int32, (half, half), 1)
        <= lax.broadcasted_iota(jnp.int32, (half, half), 0),
        0.0, NEG,
    )
    causal = jnp.concatenate([causal] * per_kv, axis=0)

    def stacked(k, top):
        rows = slice(top * half, (top + 1) * half)
        return jnp.concatenate(
            [q_v[rows, h * HEAD_SIZE:(h + 1) * HEAD_SIZE] for h in range(k * per_kv, (k + 1) * per_kv)], axis=0
        )

    units = [(k, top) for top in (0, 1) for k in range(kv_heads)]
    for number, (k, top) in enumerate(units):
        rows = slice(top * half, (top + 1) * half)
        query = stacked(k, top)
        s = dot(query, k_v[rows, key_lanes(k)], ((1,), (1,))) * scale + causal
        best = jnp.max(s, axis=1, keepdims=True)
        if top:
            s0 = dot(query, k_v[0:half, key_lanes(k)], ((1,), (1,))) * scale
            best = jnp.max(jnp.maximum(s, s0), axis=1, keepdims=True)
        value = dot(jnp.exp2(s - best).astype(jnp.bfloat16), v_v[rows, val_wide(k)])
        if top:
            value = value + dot(jnp.exp2(s0 - best).astype(jnp.bfloat16), v_v[0:half, val_wide(k)])
        acc_s[k, top] = value
        max_s[k, top] = jnp.broadcast_to(best, max_s.shape[2:])

        if number == 0:
            for source in reversed(range(1, n_ctx - 1)):
                forward_pass(source)

        @pl.when((me_c > 0) & (me_c < n_ctx - 1))
        def _():
            anchor_copy(number, False).wait_recv()
            anchor_copy(number, False).start()

        if number == kv_heads - 1 and n_ctx > 1:
            forward_pass(0)

    def await_remote(values):
        @pl.when((me_c == n_ctx - 1) & (me_c > 0))
        def _():
            for source in range(n_ctx - 1):
                copies = pass_copies(source)
                for copy in copies[1:] if values else copies[:1]:
                    copy.wait_recv()
            for k in range(kv_heads):
                anchor_copy(k + values * kv_heads, False).wait_recv()

    await_remote(0)
    place = lax.broadcasted_iota(jnp.int32, (1, rem_rows), 1)
    seen_anchor = (place < jnp.minimum(len_ref[0], ANCHOR)) & (me_c > 0)
    seen_pass = (place >= ANCHOR) & (place - ANCHOR < me_c * retained)
    bias = jnp.where(seen_anchor | seen_pass, 0.0, NEG)

    def weigh(top):
        for k in range(kv_heads):
            s = dot(stacked(k, top), rem_k[:, key_lanes(k)], ((1,), (1,))) * scale + bias
            before = max_s[k, top]
            best = jnp.maximum(before, jnp.max(s, axis=1, keepdims=True))
            wide = jnp.concatenate([best] * (rem_rows // HEAD_SIZE), axis=1)
            p_s[k, top] = jnp.exp2(s - wide).astype(jnp.bfloat16)
            fade = jnp.exp2(before - best)
            acc_s[k, top] = acc_s[k, top] * jnp.concatenate([fade, fade], axis=1)

    def attend(top):
        rows = slice(top * half, (top + 1) * half)
        for k in range(kv_heads):
            value = acc_s[k, top] + dot(p_s[k, top], rem_v[:, val_wide(k)])
            value = (value[:, :HEAD_SIZE] / value[:, HEAD_SIZE:]).astype(jnp.bfloat16)
            for g in range(per_kv):
                h = k * per_kv + g
                att[rows, h * HEAD_SIZE:(h + 1) * HEAD_SIZE] = value[g * half:(g + 1) * half]

    def red_copy(r, c, top):
        rows = pl.ds(top * half, half)
        return pltpu.make_async_remote_copy(
            src_ref=outgoing.at[r - 1, c, rows, :], dst_ref=incoming.at[r - 1, c, rows, :],
            send_sem=red_send.at[r - 1, c, top], recv_sem=red_recv.at[r - 1, c, top],
            device_id={"head": flip(me_h, low_bit(r))}, device_id_type=MESH,
        )

    def detours(i):
        return [(c, 0) for c in range(1, min(chunks, 3 - i))]

    def to_relay(i, c, top):
        return pltpu.make_async_remote_copy(
            src_ref=outgoing.at[middle - 1, c, pl.ds(top * half, half), :], dst_ref=relay.at[c - 1],
            send_sem=red_send.at[middle - 1, c, top], recv_sem=relay_recv.at[c - 1],
            device_id={"ctx": i}, device_id_type=MESH,
        )

    def from_relay(i, c, top):
        return pltpu.make_async_remote_copy(
            src_ref=relay.at[c - 1], dst_ref=incoming.at[middle - 1, c, pl.ds(top * half, half), :],
            send_sem=relay_send.at[c - 1], recv_sem=red_recv.at[middle - 1, c, top],
            device_id={"ctx": n_ctx - 1 - i, "head": flip(me_h, middle)}, device_id_type=MESH,
        )

    def pass_on():
        for i in range(pairs):
            @pl.when(me_c == i)
            def _():
                for c, top in detours(i):
                    to_relay(i, c, top).wait_recv()
                    from_relay(i, c, top).start()

    def product(r, c, rows):
        return dot(att[rows, :], w_v[r, :, c * chunk:(c + 1) * chunk])

    def with_received(total, r, c, top, first, last):
        bit = first
        while bit < last:
            red_copy(r + bit, c, top).wait_recv()
            total = total + incoming[r + bit - 1, c, top * half:(top + 1) * half, :].astype(jnp.float32)
            bit *= 2
        return total

    def send(total, r, c, top):
        outgoing[r - 1, c, top * half:(top + 1) * half, :] = total.astype(jnp.bfloat16)
        takers = [i for i in range(pairs) if r == middle and (c, top) in detours(i)]
        for i in takers:
            @pl.when(me_c == n_ctx - 1 - i)
            def _():
                to_relay(i, c, top).start()
        if takers:
            @pl.when(me_c < n_ctx - len(takers))
            def _():
                red_copy(r, c, top).start()
        else:
            red_copy(r, c, top).start()

    for r in range(middle, n_head):
        w_loads[r].wait()
    for top in (0, 1):
        rows = slice(top * half, (top + 1) * half)
        weigh(top)
        if top == 0:
            await_remote(1)
        attend(top)
        late = []
        for c in range(chunks):
            for r in reversed(range(middle, n_head)):
                value = product(r, c, rows)
                if r % 2:
                    send(value, r, c, top)
                else:
                    late.append((value, r, c))
            while len(late) > LAG:
                value, r, d = late.pop(0)
                send(with_received(value, r, d, top, 1, low_bit(r)), r, d, top)
        for value, r, d in late:
            send(with_received(value, r, d, top, 1, low_bit(r)), r, d, top)

    for r in range(middle):
        w_loads[r].wait()
    for r in reversed(range(1, middle)):
        for c in range(chunks):
            value = product(r, c, slice(0, tok))
            for top in (0, 1):
                send(with_received(value[top * half:(top + 1) * half], r, c, top, 1, low_bit(r)), r, c, top)
    for c in range(chunks):
        part[c] = product(0, c, slice(0, tok))
    for c in range(chunks):
        for top in (0, 1):
            rows = slice(top * half, (top + 1) * half)
            part[c, rows, :] = with_received(part[c, rows, :], 0, c, top, 1, middle)
    for top in (0, 1):
        rows = slice(top * half, (top + 1) * half)
        for c in range(chunks):
            if top == 1 and c == chunks // 2:
                pass_on()
            total = with_received(part[c, rows, :], 0, c, top, middle, n_head)
            o_ref[rows, c * chunk:(c + 1) * chunk] = total.astype(jnp.bfloat16)

    for r in range(1, n_head):
        for c in range(chunks):
            for top in (0, 1):
                red_copy(r, c, top).wait_send()
    for i in range(pairs):
        @pl.when(me_c == i)
        def _():
            for c, top in detours(i):
                from_relay(i, c, top).wait_send()
    @pl.when(me_c < n_ctx - 1)
    def _():
        for i in range(pieces):
            anchor_copy(i, True).wait_send()
    for source in range(n_ctx - 1):
        @pl.when((me_c >= source) & (me_c < n_ctx - 1))
        def _():
            for copy in pass_copies(source):
                copy.wait_send()


def local(n_ctx, n_head, queries, rotated_key_rows, value_state_rows, retained_positions, anchor_length, out_proj):
    tok, q_width = queries.shape
    kv_width = rotated_key_rows.shape[1]
    retained = retained_positions.shape[1]
    rem_rows = pl.cdiv(ANCHOR + n_ctx * retained, HEAD_SIZE) * HEAD_SIZE
    slab = out_proj.shape[1] // n_head
    chunk = math.gcd(slab, 256)
    chunks = slab // chunk
    dma = pltpu.SemaphoreType.DMA
    held = pl.BlockSpec(memory_space=pltpu.HBM)
    per_kv = q_width // kv_width
    kv_heads = kv_width // HEAD_SIZE
    stack = per_kv * tok // 2
    operands = [
        pltpu.with_memory_space_constraint(array, pltpu.HBM)
        for array in (retained_positions, queries, rotated_key_rows, value_state_rows, out_proj)
    ]
    return pl.pallas_call(
        functools.partial(kernel, n_ctx, n_head),
        out_shape=jax.ShapeDtypeStruct((tok, slab), jnp.bfloat16),
        in_specs=[pl.BlockSpec(memory_space=pltpu.SMEM), held, held, held, held, held],
        out_specs=pl.BlockSpec(memory_space=pltpu.VMEM),
        scratch_shapes=[
            pltpu.VMEM((1, retained), jnp.int32),
            pltpu.VMEM((tok, q_width), jnp.bfloat16),
            pltpu.VMEM((tok, kv_width), jnp.bfloat16),
            pltpu.VMEM((tok, 2 * kv_width), jnp.bfloat16),
            pltpu.VMEM((rem_rows, kv_width), jnp.bfloat16),
            pltpu.VMEM((rem_rows, 2 * kv_width), jnp.bfloat16),
            pltpu.VMEM((n_head, q_width, slab), jnp.bfloat16),
            pltpu.VMEM((kv_heads, 2, stack, 2 * HEAD_SIZE), jnp.float32),
            pltpu.VMEM((kv_heads, 2, stack, HEAD_SIZE), jnp.float32),
            pltpu.VMEM((kv_heads, 2, stack, rem_rows), jnp.bfloat16),
            pltpu.VMEM((tok, q_width), jnp.bfloat16),
            pltpu.VMEM((chunks, tok, chunk), jnp.float32),
            pltpu.VMEM((n_head - 1, chunks, tok, chunk), jnp.bfloat16),
            pltpu.VMEM((n_head - 1, chunks, tok, chunk), jnp.bfloat16),
            pltpu.VMEM((2, tok // 2, chunk), jnp.bfloat16),
            dma((3 + kv_heads,)),
            dma((n_head,)),
            dma((n_ctx, 1 + kv_heads)),
            dma((n_ctx, 1 + kv_heads)),
            dma((2 * kv_heads,)),
            dma((2 * kv_heads,)),
            dma((n_head - 1, chunks, 2)),
            dma((n_head - 1, chunks, 2)),
            dma((2,)),
            dma((2,)),
        ],
        compiler_params=pltpu.CompilerParams(
            collective_id=0, has_side_effects=True, vmem_limit_bytes=48 * 1024 * 1024
        ),
    )(anchor_length, *operands)


def solution(mesh):
    placed = (
        P(("groups", "ctx"), "head"),
        P(("groups", "ctx"), "head"),
        P(("groups", "ctx"), "head"),
        P(("groups", "ctx"), None),
        P("groups"),
        P("head", None),
    )
    return jax.shard_map(
        functools.partial(local, mesh.shape["ctx"], mesh.shape["head"]),
        mesh=mesh, in_specs=placed, out_specs=P(("groups", "ctx"), "head"), check_vma=False,
    )
```

```python
import functools
import math

import jax
import jax.numpy as jnp
from jax import lax
from jax.experimental import pallas as pl
from jax.experimental.pallas import tpu as pltpu
from jax.sharding import PartitionSpec as P

HEAD_SIZE = 128
ANCHOR = 128
MESH = pl.DeviceIdType.MESH
NEG = -1e30
LAG = 1


def flip(index, mask):
    bit = 1
    while bit <= mask:
        if mask & bit:
            index = index + bit * (1 - 2 * ((index // bit) % 2))
        bit *= 2
    return index


def low_bit(r):
    return r & -r


def dot(a, b, dims=((1,), (0,))):
    return lax.dot_general(a, b, (dims, ((), ())), preferred_element_type=jnp.float32)


def kernel(
    n_ctx, n_head, len_ref, pos_hbm, q_hbm, k_hbm, v_hbm, w_hbm, o_ref,
    pos_v, q_v, k_v, v_v, rem_k, rem_v, w_v, acc_s, max_s, p_s, att, part, outgoing, incoming,
    load_sem, w_sem, pass_send, pass_recv, anc_send, anc_recv, red_send, red_recv,
):
    me_c = lax.axis_index("ctx")
    me_h = lax.axis_index("head")
    tok, q_width = q_v.shape
    kv_width = k_v.shape[1]
    kv_heads = kv_width // HEAD_SIZE
    per_kv = q_width // kv_width
    retained = pos_v.shape[1]
    rem_rows = rem_k.shape[0]
    chunks, _, chunk = part.shape
    slab = chunks * chunk
    half = tok // 2
    pieces = 2 * kv_heads

    def key_lanes(k):
        return pl.ds(k * HEAD_SIZE, HEAD_SIZE)

    def val_lanes(k):
        return pl.ds(2 * k * HEAD_SIZE, HEAD_SIZE)

    def val_wide(k):
        return pl.ds(2 * k * HEAD_SIZE, 2 * HEAD_SIZE)

    loads = [pltpu.make_async_copy(k_hbm, k_v, load_sem.at[0])]
    loads += [
        pltpu.make_async_copy(v_hbm.at[:, key_lanes(k)], v_v.at[:, val_lanes(k)], load_sem.at[3 + k])
        for k in range(kv_heads)
    ]
    loads.append(pltpu.make_async_copy(pos_hbm, pos_v, load_sem.at[1]))
    load_q = pltpu.make_async_copy(q_hbm, q_v, load_sem.at[2])
    for copy in loads:
        copy.start()
    load_q.start()

    rem_k[...] = jnp.zeros_like(rem_k)
    for k in range(kv_heads):
        ones = slice((2 * k + 1) * HEAD_SIZE, (2 * k + 2) * HEAD_SIZE)
        v_v[:, ones] = jnp.ones((tok, HEAD_SIZE), jnp.bfloat16)
        rem_v[:, ones] = jnp.ones((rem_rows, HEAD_SIZE), jnp.bfloat16)
        rem_v[:, val_lanes(k)] = jnp.zeros((rem_rows, HEAD_SIZE), jnp.bfloat16)

    barrier = pltpu.get_barrier_semaphore()
    @pl.when(me_c > 0)
    def _():
        before = lax.rem(me_c + n_ctx - 1, n_ctx)
        pl.semaphore_signal(barrier, inc=1, device_id={"ctx": before}, device_id_type=MESH)
    bit, steps = 1, 0
    while bit < n_head:
        pl.semaphore_signal(barrier, inc=1, device_id={"head": flip(me_h, bit)}, device_id_type=MESH)
        bit, steps = 2 * bit, steps + 1

    w_loads = {}
    for r in reversed(range(n_head)):
        columns = pl.ds(pl.multiple_of(flip(me_h, r) * slab, slab), slab)
        w_loads[r] = pltpu.make_async_copy(w_hbm.at[:, columns], w_v.at[r], w_sem.at[r])
        w_loads[r].start()

    def pass_copies(source):
        rows = pl.ds(pl.multiple_of(ANCHOR + source * retained, retained), retained)
        refs = [rem_k.at[rows, :]] + [rem_v.at[rows, val_lanes(k)] for k in range(kv_heads)]
        return [
            pltpu.make_async_remote_copy(
                src_ref=ref, dst_ref=ref,
                send_sem=pass_send.at[source, i], recv_sem=pass_recv.at[source, i],
                device_id={"ctx": lax.rem(me_c + 1, n_ctx)}, device_id_type=MESH,
            )
            for i, ref in enumerate(refs)
        ]

    def anchor_copy(i, origin):
        rows = pl.ds(0, ANCHOR)
        if i < kv_heads:
            source, target, lanes = k_hbm, rem_k, key_lanes(i)
        else:
            source, target, lanes = v_hbm, rem_v, val_lanes(i - kv_heads)
        held = target.at[rows, lanes]
        return pltpu.make_async_remote_copy(
            src_ref=source.at[rows, key_lanes(i % kv_heads)] if origin else held, dst_ref=held,
            send_sem=anc_send.at[i], recv_sem=anc_recv.at[i],
            device_id={"ctx": lax.rem(me_c + 1, n_ctx)}, device_id_type=MESH,
        )

    @pl.when(me_c < n_ctx - 1)
    def _():
        pl.semaphore_wait(barrier, steps + 1)

    @pl.when(me_c == n_ctx - 1)
    def _():
        pl.semaphore_wait(barrier, steps)

    def start_anchor(first, last):
        if n_ctx > 1:
            @pl.when(me_c == 0)
            def _():
                for i in range(first, last):
                    anchor_copy(i, True).start()

    start_anchor(0, pieces)
    for copy in loads:
        copy.wait()
    picked = lax.broadcasted_iota(jnp.int32, (tok, retained), 0) == pos_v[...]
    picked = picked.astype(jnp.bfloat16)
    mine = pl.ds(pl.multiple_of(ANCHOR + me_c * retained, retained), retained)
    rem_k[mine, :] = dot(picked, k_v[...], ((0,), (0,))).astype(jnp.bfloat16)
    for k in range(kv_heads):
        rem_v[mine, val_lanes(k)] = dot(picked, v_v[:, val_lanes(k)], ((0,), (0,))).astype(jnp.bfloat16)
    @pl.when(me_c < n_ctx - 1)
    def _():
        for copy in pass_copies(me_c):
            copy.start()

    def forward_pass(source):
        @pl.when((me_c > source) & (me_c < n_ctx - 1))
        def _():
            for copy in pass_copies(source):
                copy.wait_recv()
                copy.start()

    scale = HEAD_SIZE ** -0.5 * math.log2(math.e)
    load_q.wait()

    causal = jnp.where(
        lax.broadcasted_iota(jnp.int32, (half, half), 1)
        <= lax.broadcasted_iota(jnp.int32, (half, half), 0),
        0.0, NEG,
    )
    causal = jnp.concatenate([causal] * per_kv, axis=0)

    def stacked(k, top):
        rows = slice(top * half, (top + 1) * half)
        return jnp.concatenate(
            [q_v[rows, h * HEAD_SIZE:(h + 1) * HEAD_SIZE] for h in range(k * per_kv, (k + 1) * per_kv)], axis=0
        )

    units = [(k, top) for top in (0, 1) for k in range(kv_heads)]
    for number, (k, top) in enumerate(units):
        if number == 0:
            for source in reversed(range(1, n_ctx - 1)):
                forward_pass(source)

        @pl.when((me_c > 0) & (me_c < n_ctx - 1))
        def _():
            anchor_copy(number, False).wait_recv()
            anchor_copy(number, False).start()

        if number == kv_heads - 1 and n_ctx > 1:
            forward_pass(0)

        rows = slice(top * half, (top + 1) * half)
        query = stacked(k, top)
        s = dot(query, k_v[rows, key_lanes(k)], ((1,), (1,))) * scale + causal
        best = jnp.max(s, axis=1, keepdims=True)
        if top:
            s0 = dot(query, k_v[0:half, key_lanes(k)], ((1,), (1,))) * scale
            best = jnp.max(jnp.maximum(s, s0), axis=1, keepdims=True)
        value = dot(jnp.exp2(s - best).astype(jnp.bfloat16), v_v[rows, val_wide(k)])
        if top:
            value = value + dot(jnp.exp2(s0 - best).astype(jnp.bfloat16), v_v[0:half, val_wide(k)])
        acc_s[k, top] = value
        max_s[k, top] = jnp.broadcast_to(best, max_s.shape[2:])

    def await_remote(values):
        @pl.when((me_c == n_ctx - 1) & (me_c > 0))
        def _():
            for source in range(n_ctx - 1):
                copies = pass_copies(source)
                for copy in copies[1:] if values else copies[:1]:
                    copy.wait_recv()
            for k in range(kv_heads):
                anchor_copy(k + values * kv_heads, False).wait_recv()

    await_remote(0)
    place = lax.broadcasted_iota(jnp.int32, (1, rem_rows), 1)
    seen_anchor = (place < jnp.minimum(len_ref[0], ANCHOR)) & (me_c > 0)
    seen_pass = (place >= ANCHOR) & (place - ANCHOR < me_c * retained)
    bias = jnp.where(seen_anchor | seen_pass, 0.0, NEG)

    def weigh(top):
        for k in range(kv_heads):
            s = dot(stacked(k, top), rem_k[:, key_lanes(k)], ((1,), (1,))) * scale + bias
            before = max_s[k, top]
            best = jnp.maximum(before, jnp.max(s, axis=1, keepdims=True))
            wide = jnp.concatenate([best] * (rem_rows // HEAD_SIZE), axis=1)
            p_s[k, top] = jnp.exp2(s - wide).astype(jnp.bfloat16)
            fade = jnp.exp2(before - best)
            acc_s[k, top] = acc_s[k, top] * jnp.concatenate([fade, fade], axis=1)

    def attend(top):
        rows = slice(top * half, (top + 1) * half)
        for k in range(kv_heads):
            value = acc_s[k, top] + dot(p_s[k, top], rem_v[:, val_wide(k)])
            value = (value[:, :HEAD_SIZE] / value[:, HEAD_SIZE:]).astype(jnp.bfloat16)
            for g in range(per_kv):
                h = k * per_kv + g
                att[rows, h * HEAD_SIZE:(h + 1) * HEAD_SIZE] = value[g * half:(g + 1) * half]

    def red_copy(r, c, top):
        rows = pl.ds(top * half, half)
        return pltpu.make_async_remote_copy(
            src_ref=outgoing.at[r - 1, c, rows, :], dst_ref=incoming.at[r - 1, c, rows, :],
            send_sem=red_send.at[r - 1, c, top], recv_sem=red_recv.at[r - 1, c, top],
            device_id={"head": flip(me_h, low_bit(r))}, device_id_type=MESH,
        )

    def product(r, c, rows):
        return dot(att[rows, :], w_v[r, :, c * chunk:(c + 1) * chunk])

    def with_received(total, r, c, top, first, last):
        bit = first
        while bit < last:
            red_copy(r + bit, c, top).wait_recv()
            total = total + incoming[r + bit - 1, c, top * half:(top + 1) * half, :].astype(jnp.float32)
            bit *= 2
        return total

    def send(total, r, c, top):
        outgoing[r - 1, c, top * half:(top + 1) * half, :] = total.astype(jnp.bfloat16)
        red_copy(r, c, top).start()

    middle = n_head // 2
    for r in range(middle, n_head):
        w_loads[r].wait()
    for top in (0, 1):
        rows = slice(top * half, (top + 1) * half)
        weigh(top)
        if top == 0:
            await_remote(1)
        attend(top)
        late = []
        for c in range(chunks):
            for r in reversed(range(middle, n_head)):
                value = product(r, c, rows)
                if r % 2:
                    send(value, r, c, top)
                else:
                    late.append((value, r, c))
            while len(late) > LAG:
                value, r, d = late.pop(0)
                send(with_received(value, r, d, top, 1, low_bit(r)), r, d, top)
        for value, r, d in late:
            send(with_received(value, r, d, top, 1, low_bit(r)), r, d, top)

    for r in range(middle):
        w_loads[r].wait()
    for r in reversed(range(1, middle)):
        for c in range(chunks):
            value = product(r, c, slice(0, tok))
            for top in (0, 1):
                send(with_received(value[top * half:(top + 1) * half], r, c, top, 1, low_bit(r)), r, c, top)
    for c in range(chunks):
        part[c] = product(0, c, slice(0, tok))
    for c in range(chunks):
        for top in (0, 1):
            rows = slice(top * half, (top + 1) * half)
            part[c, rows, :] = with_received(part[c, rows, :], 0, c, top, 1, middle)
    for top in (0, 1):
        rows = slice(top * half, (top + 1) * half)
        for c in range(chunks):
            total = with_received(part[c, rows, :], 0, c, top, middle, n_head)
            o_ref[rows, c * chunk:(c + 1) * chunk] = total.astype(jnp.bfloat16)

    for r in range(1, n_head):
        for c in range(chunks):
            for top in (0, 1):
                red_copy(r, c, top).wait_send()
    @pl.when(me_c < n_ctx - 1)
    def _():
        for i in range(pieces):
            anchor_copy(i, True).wait_send()
    for source in range(n_ctx - 1):
        @pl.when((me_c >= source) & (me_c < n_ctx - 1))
        def _():
            for copy in pass_copies(source):
                copy.wait_send()


def local(n_ctx, n_head, queries, rotated_key_rows, value_state_rows, retained_positions, anchor_length, out_proj):
    tok, q_width = queries.shape
    kv_width = rotated_key_rows.shape[1]
    retained = retained_positions.shape[1]
    rem_rows = pl.cdiv(ANCHOR + n_ctx * retained, HEAD_SIZE) * HEAD_SIZE
    slab = out_proj.shape[1] // n_head
    chunk = math.gcd(slab, 256)
    chunks = slab // chunk
    dma = pltpu.SemaphoreType.DMA
    held = pl.BlockSpec(memory_space=pltpu.HBM)
    per_kv = q_width // kv_width
    kv_heads = kv_width // HEAD_SIZE
    stack = per_kv * tok // 2
    operands = [
        pltpu.with_memory_space_constraint(array, pltpu.HBM)
        for array in (retained_positions, queries, rotated_key_rows, value_state_rows, out_proj)
    ]
    return pl.pallas_call(
        functools.partial(kernel, n_ctx, n_head),
        out_shape=jax.ShapeDtypeStruct((tok, slab), jnp.bfloat16),
        in_specs=[pl.BlockSpec(memory_space=pltpu.SMEM), held, held, held, held, held],
        out_specs=pl.BlockSpec(memory_space=pltpu.VMEM),
        scratch_shapes=[
            pltpu.VMEM((1, retained), jnp.int32),
            pltpu.VMEM((tok, q_width), jnp.bfloat16),
            pltpu.VMEM((tok, kv_width), jnp.bfloat16),
            pltpu.VMEM((tok, 2 * kv_width), jnp.bfloat16),
            pltpu.VMEM((rem_rows, kv_width), jnp.bfloat16),
            pltpu.VMEM((rem_rows, 2 * kv_width), jnp.bfloat16),
            pltpu.VMEM((n_head, q_width, slab), jnp.bfloat16),
            pltpu.VMEM((kv_heads, 2, stack, 2 * HEAD_SIZE), jnp.float32),
            pltpu.VMEM((kv_heads, 2, stack, HEAD_SIZE), jnp.float32),
            pltpu.VMEM((kv_heads, 2, stack, rem_rows), jnp.bfloat16),
            pltpu.VMEM((tok, q_width), jnp.bfloat16),
            pltpu.VMEM((chunks, tok, chunk), jnp.float32),
            pltpu.VMEM((n_head - 1, chunks, tok, chunk), jnp.bfloat16),
            pltpu.VMEM((n_head - 1, chunks, tok, chunk), jnp.bfloat16),
            dma((3 + kv_heads,)),
            dma((n_head,)),
            dma((n_ctx, 1 + kv_heads)),
            dma((n_ctx, 1 + kv_heads)),
            dma((2 * kv_heads,)),
            dma((2 * kv_heads,)),
            dma((n_head - 1, chunks, 2)),
            dma((n_head - 1, chunks, 2)),
        ],
        compiler_params=pltpu.CompilerParams(
            collective_id=0, has_side_effects=True, vmem_limit_bytes=48 * 1024 * 1024
        ),
    )(anchor_length, *operands)


def solution(mesh):
    placed = (
        P(("groups", "ctx"), "head"),
        P(("groups", "ctx"), "head"),
        P(("groups", "ctx"), "head"),
        P(("groups", "ctx"), None),
        P("groups"),
        P("head", None),
    )
    return jax.shard_map(
        functools.partial(local, mesh.shape["ctx"], mesh.shape["head"]),
        mesh=mesh, in_specs=placed, out_specs=P(("groups", "ctx"), "head"), check_vma=False,
    )
```

```python
import functools
import math

import jax
import jax.numpy as jnp
from jax import lax
from jax.experimental import pallas as pl
from jax.experimental.pallas import tpu as pltpu
from jax.sharding import PartitionSpec as P

HEAD_SIZE = 128
ANCHOR = 128
MESH = pl.DeviceIdType.MESH
NEG = -1e30
LAG = 1


def flip(index, mask):
    bit = 1
    while bit <= mask:
        if mask & bit:
            index = index + bit * (1 - 2 * ((index // bit) % 2))
        bit *= 2
    return index


def low_bit(r):
    return r & -r


def dot(a, b, dims=((1,), (0,))):
    return lax.dot_general(a, b, (dims, ((), ())), preferred_element_type=jnp.float32)


def kernel(
    n_ctx, n_head, len_ref, pos_hbm, q_hbm, k_hbm, v_hbm, w_hbm, o_ref,
    pos_v, q_v, k_v, v_v, rem_k, rem_v, w_v, acc_s, max_s, p_s, att, part, outgoing, incoming,
    load_sem, w_sem, pass_send, pass_recv, anc_send, anc_recv, red_send, red_recv,
):
    me_c = lax.axis_index("ctx")
    me_h = lax.axis_index("head")
    tok, q_width = q_v.shape
    kv_width = k_v.shape[1]
    kv_heads = kv_width // HEAD_SIZE
    per_kv = q_width // kv_width
    retained = pos_v.shape[1]
    rem_rows = rem_k.shape[0]
    chunks, _, chunk = part.shape
    slab = chunks * chunk
    half = tok // 2
    pieces = 2 * kv_heads

    def key_lanes(k):
        return pl.ds(k * HEAD_SIZE, HEAD_SIZE)

    def val_lanes(k):
        return pl.ds(2 * k * HEAD_SIZE, HEAD_SIZE)

    def val_wide(k):
        return pl.ds(2 * k * HEAD_SIZE, 2 * HEAD_SIZE)

    loads = [pltpu.make_async_copy(k_hbm, k_v, load_sem.at[0])]
    loads += [
        pltpu.make_async_copy(v_hbm.at[:, key_lanes(k)], v_v.at[:, val_lanes(k)], load_sem.at[3 + k])
        for k in range(kv_heads)
    ]
    loads.append(pltpu.make_async_copy(pos_hbm, pos_v, load_sem.at[1]))
    load_q = pltpu.make_async_copy(q_hbm, q_v, load_sem.at[2])
    for copy in loads:
        copy.start()
    load_q.start()

    rem_k[...] = jnp.zeros_like(rem_k)
    for k in range(kv_heads):
        ones = slice((2 * k + 1) * HEAD_SIZE, (2 * k + 2) * HEAD_SIZE)
        v_v[:, ones] = jnp.ones((tok, HEAD_SIZE), jnp.bfloat16)
        rem_v[:, ones] = jnp.ones((rem_rows, HEAD_SIZE), jnp.bfloat16)
        rem_v[:, val_lanes(k)] = jnp.zeros((rem_rows, HEAD_SIZE), jnp.bfloat16)

    barrier = pltpu.get_barrier_semaphore()
    @pl.when(me_c > 0)
    def _():
        before = lax.rem(me_c + n_ctx - 1, n_ctx)
        pl.semaphore_signal(barrier, inc=1, device_id={"ctx": before}, device_id_type=MESH)
    bit, steps = 1, 0
    while bit < n_head:
        pl.semaphore_signal(barrier, inc=1, device_id={"head": flip(me_h, bit)}, device_id_type=MESH)
        bit, steps = 2 * bit, steps + 1

    w_loads = {}
    for r in reversed(range(n_head)):
        columns = pl.ds(pl.multiple_of(flip(me_h, r) * slab, slab), slab)
        w_loads[r] = pltpu.make_async_copy(w_hbm.at[:, columns], w_v.at[r], w_sem.at[r])
        w_loads[r].start()

    def pass_copies(source):
        rows = pl.ds(pl.multiple_of(ANCHOR + source * retained, retained), retained)
        refs = [rem_k.at[rows, :]] + [rem_v.at[rows, val_lanes(k)] for k in range(kv_heads)]
        return [
            pltpu.make_async_remote_copy(
                src_ref=ref, dst_ref=ref,
                send_sem=pass_send.at[source, i], recv_sem=pass_recv.at[source, i],
                device_id={"ctx": lax.rem(me_c + 1, n_ctx)}, device_id_type=MESH,
            )
            for i, ref in enumerate(refs)
        ]

    def anchor_copy(i, origin):
        rows = pl.ds(0, ANCHOR)
        if i < kv_heads:
            source, target, lanes = k_hbm, rem_k, key_lanes(i)
        else:
            source, target, lanes = v_v, rem_v, val_lanes(i - kv_heads)
        return pltpu.make_async_remote_copy(
            src_ref=(source if origin else target).at[rows, lanes], dst_ref=target.at[rows, lanes],
            send_sem=anc_send.at[i], recv_sem=anc_recv.at[i],
            device_id={"ctx": lax.rem(me_c + 1, n_ctx)}, device_id_type=MESH,
        )

    @pl.when(me_c < n_ctx - 1)
    def _():
        pl.semaphore_wait(barrier, steps + 1)

    @pl.when(me_c == n_ctx - 1)
    def _():
        pl.semaphore_wait(barrier, steps)

    def start_anchor(first, last):
        if n_ctx > 1:
            @pl.when(me_c == 0)
            def _():
                for i in range(first, last):
                    anchor_copy(i, True).start()

    start_anchor(0, kv_heads)
    for copy in loads:
        copy.wait()
    picked = lax.broadcasted_iota(jnp.int32, (tok, retained), 0) == pos_v[...]
    picked = picked.astype(jnp.bfloat16)
    mine = pl.ds(pl.multiple_of(ANCHOR + me_c * retained, retained), retained)
    rem_k[mine, :] = dot(picked, k_v[...], ((0,), (0,))).astype(jnp.bfloat16)
    for k in range(kv_heads):
        rem_v[mine, val_lanes(k)] = dot(picked, v_v[:, val_lanes(k)], ((0,), (0,))).astype(jnp.bfloat16)
    @pl.when(me_c < n_ctx - 1)
    def _():
        for copy in pass_copies(me_c):
            copy.start()

    start_anchor(kv_heads, pieces)

    def forward_pass(source):
        @pl.when((me_c > source) & (me_c < n_ctx - 1))
        def _():
            for copy in pass_copies(source):
                copy.wait_recv()
                copy.start()

    scale = HEAD_SIZE ** -0.5 * math.log2(math.e)
    load_q.wait()

    causal = jnp.where(
        lax.broadcasted_iota(jnp.int32, (half, half), 1)
        <= lax.broadcasted_iota(jnp.int32, (half, half), 0),
        0.0, NEG,
    )
    causal = jnp.concatenate([causal] * per_kv, axis=0)

    def stacked(k, top):
        rows = slice(top * half, (top + 1) * half)
        return jnp.concatenate(
            [q_v[rows, h * HEAD_SIZE:(h + 1) * HEAD_SIZE] for h in range(k * per_kv, (k + 1) * per_kv)], axis=0
        )

    units = [(k, top) for top in (0, 1) for k in range(kv_heads)]
    for number, (k, top) in enumerate(units):
        rows = slice(top * half, (top + 1) * half)
        query = stacked(k, top)
        s = dot(query, k_v[rows, key_lanes(k)], ((1,), (1,))) * scale + causal
        best = jnp.max(s, axis=1, keepdims=True)
        if top:
            s0 = dot(query, k_v[0:half, key_lanes(k)], ((1,), (1,))) * scale
            best = jnp.max(jnp.maximum(s, s0), axis=1, keepdims=True)
        value = dot(jnp.exp2(s - best).astype(jnp.bfloat16), v_v[rows, val_wide(k)])
        if top:
            value = value + dot(jnp.exp2(s0 - best).astype(jnp.bfloat16), v_v[0:half, val_wide(k)])
        acc_s[k, top] = value
        max_s[k, top] = jnp.broadcast_to(best, max_s.shape[2:])

        if number == 0:
            for source in reversed(range(1, n_ctx - 1)):
                forward_pass(source)

        @pl.when((me_c > 0) & (me_c < n_ctx - 1))
        def _():
            anchor_copy(number, False).wait_recv()
            anchor_copy(number, False).start()

        if number == kv_heads - 1 and n_ctx > 1:
            forward_pass(0)

    def await_remote(values):
        @pl.when((me_c == n_ctx - 1) & (me_c > 0))
        def _():
            for source in range(n_ctx - 1):
                copies = pass_copies(source)
                for copy in copies[1:] if values else copies[:1]:
                    copy.wait_recv()
            for k in range(kv_heads):
                anchor_copy(k + values * kv_heads, False).wait_recv()

    await_remote(0)
    place = lax.broadcasted_iota(jnp.int32, (1, rem_rows), 1)
    seen_anchor = (place < jnp.minimum(len_ref[0], ANCHOR)) & (me_c > 0)
    seen_pass = (place >= ANCHOR) & (place - ANCHOR < me_c * retained)
    bias = jnp.where(seen_anchor | seen_pass, 0.0, NEG)

    def weigh(top):
        for k in range(kv_heads):
            s = dot(stacked(k, top), rem_k[:, key_lanes(k)], ((1,), (1,))) * scale + bias
            before = max_s[k, top]
            best = jnp.maximum(before, jnp.max(s, axis=1, keepdims=True))
            wide = jnp.concatenate([best] * (rem_rows // HEAD_SIZE), axis=1)
            p_s[k, top] = jnp.exp2(s - wide).astype(jnp.bfloat16)
            fade = jnp.exp2(before - best)
            acc_s[k, top] = acc_s[k, top] * jnp.concatenate([fade, fade], axis=1)

    def attend(top):
        rows = slice(top * half, (top + 1) * half)
        for k in range(kv_heads):
            value = acc_s[k, top] + dot(p_s[k, top], rem_v[:, val_wide(k)])
            value = (value[:, :HEAD_SIZE] / value[:, HEAD_SIZE:]).astype(jnp.bfloat16)
            for g in range(per_kv):
                h = k * per_kv + g
                att[rows, h * HEAD_SIZE:(h + 1) * HEAD_SIZE] = value[g * half:(g + 1) * half]

    def red_copy(r, c, top):
        rows = pl.ds(top * half, half)
        return pltpu.make_async_remote_copy(
            src_ref=outgoing.at[r - 1, c, rows, :], dst_ref=incoming.at[r - 1, c, rows, :],
            send_sem=red_send.at[r - 1, c, top], recv_sem=red_recv.at[r - 1, c, top],
            device_id={"head": flip(me_h, low_bit(r))}, device_id_type=MESH,
        )

    def product(r, c, rows):
        return dot(att[rows, :], w_v[r, :, c * chunk:(c + 1) * chunk])

    def with_received(total, r, c, top, first, last):
        bit = first
        while bit < last:
            red_copy(r + bit, c, top).wait_recv()
            total = total + incoming[r + bit - 1, c, top * half:(top + 1) * half, :].astype(jnp.float32)
            bit *= 2
        return total

    def send(total, r, c, top):
        outgoing[r - 1, c, top * half:(top + 1) * half, :] = total.astype(jnp.bfloat16)
        red_copy(r, c, top).start()

    middle = n_head // 2
    for r in range(middle, n_head):
        w_loads[r].wait()
    for top in (0, 1):
        rows = slice(top * half, (top + 1) * half)
        weigh(top)
        if top == 0:
            await_remote(1)
        attend(top)
        late = []
        for c in range(chunks):
            for r in reversed(range(middle, n_head)):
                value = product(r, c, rows)
                if r % 2:
                    send(value, r, c, top)
                else:
                    late.append((value, r, c))
            while len(late) > LAG:
                value, r, d = late.pop(0)
                send(with_received(value, r, d, top, 1, low_bit(r)), r, d, top)
        for value, r, d in late:
            send(with_received(value, r, d, top, 1, low_bit(r)), r, d, top)

    for r in range(middle):
        w_loads[r].wait()
    for r in reversed(range(1, middle)):
        for c in range(chunks):
            value = product(r, c, slice(0, tok))
            for top in (0, 1):
                send(with_received(value[top * half:(top + 1) * half], r, c, top, 1, low_bit(r)), r, c, top)
    for c in range(chunks):
        part[c] = product(0, c, slice(0, tok))
    for c in range(chunks):
        for top in (0, 1):
            rows = slice(top * half, (top + 1) * half)
            part[c, rows, :] = with_received(part[c, rows, :], 0, c, top, 1, middle)
    for top in (0, 1):
        rows = slice(top * half, (top + 1) * half)
        for c in range(chunks):
            total = with_received(part[c, rows, :], 0, c, top, middle, n_head)
            o_ref[rows, c * chunk:(c + 1) * chunk] = total.astype(jnp.bfloat16)

    for r in range(1, n_head):
        for c in range(chunks):
            for top in (0, 1):
                red_copy(r, c, top).wait_send()
    @pl.when(me_c < n_ctx - 1)
    def _():
        for i in range(pieces):
            anchor_copy(i, True).wait_send()
    for source in range(n_ctx - 1):
        @pl.when((me_c >= source) & (me_c < n_ctx - 1))
        def _():
            for copy in pass_copies(source):
                copy.wait_send()


def local(n_ctx, n_head, queries, rotated_key_rows, value_state_rows, retained_positions, anchor_length, out_proj):
    tok, q_width = queries.shape
    kv_width = rotated_key_rows.shape[1]
    retained = retained_positions.shape[1]
    rem_rows = pl.cdiv(ANCHOR + n_ctx * retained, HEAD_SIZE) * HEAD_SIZE
    slab = out_proj.shape[1] // n_head
    chunk = math.gcd(slab, 256)
    chunks = slab // chunk
    dma = pltpu.SemaphoreType.DMA
    held = pl.BlockSpec(memory_space=pltpu.HBM)
    per_kv = q_width // kv_width
    kv_heads = kv_width // HEAD_SIZE
    stack = per_kv * tok // 2
    operands = [
        pltpu.with_memory_space_constraint(array, pltpu.HBM)
        for array in (retained_positions, queries, rotated_key_rows, value_state_rows, out_proj)
    ]
    return pl.pallas_call(
        functools.partial(kernel, n_ctx, n_head),
        out_shape=jax.ShapeDtypeStruct((tok, slab), jnp.bfloat16),
        in_specs=[pl.BlockSpec(memory_space=pltpu.SMEM), held, held, held, held, held],
        out_specs=pl.BlockSpec(memory_space=pltpu.VMEM),
        scratch_shapes=[
            pltpu.VMEM((1, retained), jnp.int32),
            pltpu.VMEM((tok, q_width), jnp.bfloat16),
            pltpu.VMEM((tok, kv_width), jnp.bfloat16),
            pltpu.VMEM((tok, 2 * kv_width), jnp.bfloat16),
            pltpu.VMEM((rem_rows, kv_width), jnp.bfloat16),
            pltpu.VMEM((rem_rows, 2 * kv_width), jnp.bfloat16),
            pltpu.VMEM((n_head, q_width, slab), jnp.bfloat16),
            pltpu.VMEM((kv_heads, 2, stack, 2 * HEAD_SIZE), jnp.float32),
            pltpu.VMEM((kv_heads, 2, stack, HEAD_SIZE), jnp.float32),
            pltpu.VMEM((kv_heads, 2, stack, rem_rows), jnp.bfloat16),
            pltpu.VMEM((tok, q_width), jnp.bfloat16),
            pltpu.VMEM((chunks, tok, chunk), jnp.float32),
            pltpu.VMEM((n_head - 1, chunks, tok, chunk), jnp.bfloat16),
            pltpu.VMEM((n_head - 1, chunks, tok, chunk), jnp.bfloat16),
            dma((3 + kv_heads,)),
            dma((n_head,)),
            dma((n_ctx, 1 + kv_heads)),
            dma((n_ctx, 1 + kv_heads)),
            dma((2 * kv_heads,)),
            dma((2 * kv_heads,)),
            dma((n_head - 1, chunks, 2)),
            dma((n_head - 1, chunks, 2)),
        ],
        compiler_params=pltpu.CompilerParams(
            collective_id=0, has_side_effects=True, vmem_limit_bytes=48 * 1024 * 1024
        ),
    )(anchor_length, *operands)


def solution(mesh):
    placed = (
        P(("groups", "ctx"), "head"),
        P(("groups", "ctx"), "head"),
        P(("groups", "ctx"), "head"),
        P(("groups", "ctx"), None),
        P("groups"),
        P("head", None),
    )
    return jax.shard_map(
        functools.partial(local, mesh.shape["ctx"], mesh.shape["head"]),
        mesh=mesh, in_specs=placed, out_specs=P(("groups", "ctx"), "head"), check_vma=False,
    )
```

```python
import functools
import math

import jax
import jax.numpy as jnp
from jax import lax
from jax.experimental import pallas as pl
from jax.experimental.pallas import tpu as pltpu
from jax.sharding import PartitionSpec as P

HEAD_SIZE = 128
ANCHOR = 128
MESH = pl.DeviceIdType.MESH
NEG = -1e30
LAG = 1


def flip(index, mask):
    bit = 1
    while bit <= mask:
        if mask & bit:
            index = index + bit * (1 - 2 * ((index // bit) % 2))
        bit *= 2
    return index


def low_bit(r):
    return r & -r


def dot(a, b, dims=((1,), (0,))):
    return lax.dot_general(a, b, (dims, ((), ())), preferred_element_type=jnp.float32)


def kernel(
    n_ctx, n_head, len_ref, pos_hbm, q_hbm, k_hbm, v_hbm, w_hbm, o_ref,
    pos_v, q_v, k_v, v_v, rem_k, rem_v, w_v, acc_s, max_s, p_s, att, part, outgoing, incoming,
    load_sem, w_sem, pass_send, pass_recv, anc_send, anc_recv, red_send, red_recv,
):
    me_c = lax.axis_index("ctx")
    me_h = lax.axis_index("head")
    tok, q_width = q_v.shape
    kv_width = k_v.shape[1]
    kv_heads = kv_width // HEAD_SIZE
    per_kv = q_width // kv_width
    retained = pos_v.shape[1]
    rem_rows = rem_k.shape[0]
    chunks, _, chunk = part.shape
    slab = chunks * chunk
    half = tok // 2
    pieces = 3 * kv_heads

    def key_lanes(k):
        return pl.ds(k * HEAD_SIZE, HEAD_SIZE)

    def val_lanes(k):
        return pl.ds(2 * k * HEAD_SIZE, HEAD_SIZE)

    def val_wide(k):
        return pl.ds(2 * k * HEAD_SIZE, 2 * HEAD_SIZE)

    loads = [pltpu.make_async_copy(k_hbm, k_v, load_sem.at[0])]
    loads += [
        pltpu.make_async_copy(v_hbm.at[:, key_lanes(k)], v_v.at[:, val_lanes(k)], load_sem.at[3 + k])
        for k in range(kv_heads)
    ]
    loads.append(pltpu.make_async_copy(pos_hbm, pos_v, load_sem.at[1]))
    load_q = pltpu.make_async_copy(q_hbm, q_v, load_sem.at[2])
    for copy in loads:
        copy.start()
    load_q.start()

    rem_k[...] = jnp.zeros_like(rem_k)
    for k in range(kv_heads):
        ones = slice((2 * k + 1) * HEAD_SIZE, (2 * k + 2) * HEAD_SIZE)
        v_v[:, ones] = jnp.ones((tok, HEAD_SIZE), jnp.bfloat16)
        rem_v[:, ones] = jnp.ones((rem_rows, HEAD_SIZE), jnp.bfloat16)
        rem_v[:, val_lanes(k)] = jnp.zeros((rem_rows, HEAD_SIZE), jnp.bfloat16)

    barrier = pltpu.get_barrier_semaphore()
    @pl.when(me_c > 0)
    def _():
        before = lax.rem(me_c + n_ctx - 1, n_ctx)
        pl.semaphore_signal(barrier, inc=1, device_id={"ctx": before}, device_id_type=MESH)
    bit, steps = 1, 0
    while bit < n_head:
        pl.semaphore_signal(barrier, inc=1, device_id={"head": flip(me_h, bit)}, device_id_type=MESH)
        bit, steps = 2 * bit, steps + 1

    w_loads = {}
    for r in reversed(range(n_head)):
        columns = pl.ds(pl.multiple_of(flip(me_h, r) * slab, slab), slab)
        w_loads[r] = pltpu.make_async_copy(w_hbm.at[:, columns], w_v.at[r], w_sem.at[r])
        w_loads[r].start()

    def pass_copies(source):
        rows = pl.ds(pl.multiple_of(ANCHOR + source * retained, retained), retained)
        refs = [rem_k.at[rows, :]] + [rem_v.at[rows, val_lanes(k)] for k in range(kv_heads)]
        return [
            pltpu.make_async_remote_copy(
                src_ref=ref, dst_ref=ref,
                send_sem=pass_send.at[source, i], recv_sem=pass_recv.at[source, i],
                device_id={"ctx": lax.rem(me_c + 1, n_ctx)}, device_id_type=MESH,
            )
            for i, ref in enumerate(refs)
        ]

    def anchor_copy(i, origin):
        rows = pl.ds(0, ANCHOR)
        if i < kv_heads:
            source, target, lanes = k_v, rem_k, key_lanes(i)
        else:
            source, target, lanes = v_v, rem_v, val_lanes((i - kv_heads) // 2)
            rows = pl.ds((i - kv_heads) % 2 * (ANCHOR // 2), ANCHOR // 2)
        return pltpu.make_async_remote_copy(
            src_ref=(source if origin else target).at[rows, lanes], dst_ref=target.at[rows, lanes],
            send_sem=anc_send.at[i], recv_sem=anc_recv.at[i],
            device_id={"ctx": lax.rem(me_c + 1, n_ctx)}, device_id_type=MESH,
        )

    for copy in loads:
        copy.wait()
    @pl.when(me_c < n_ctx - 1)
    def _():
        pl.semaphore_wait(barrier, steps + 1)

    @pl.when(me_c == n_ctx - 1)
    def _():
        pl.semaphore_wait(barrier, steps)

    def start_anchor(first, last):
        if n_ctx > 1:
            @pl.when(me_c == 0)
            def _():
                for i in range(first, last):
                    anchor_copy(i, True).start()

    start_anchor(0, kv_heads)
    picked = lax.broadcasted_iota(jnp.int32, (tok, retained), 0) == pos_v[...]
    picked = picked.astype(jnp.bfloat16)
    mine = pl.ds(pl.multiple_of(ANCHOR + me_c * retained, retained), retained)
    rem_k[mine, :] = dot(picked, k_v[...], ((0,), (0,))).astype(jnp.bfloat16)
    for k in range(kv_heads):
        rem_v[mine, val_lanes(k)] = dot(picked, v_v[:, val_lanes(k)], ((0,), (0,))).astype(jnp.bfloat16)
    @pl.when(me_c < n_ctx - 1)
    def _():
        for copy in pass_copies(me_c):
            copy.start()

    start_anchor(kv_heads, pieces)

    def forward_pass(source):
        @pl.when((me_c > source) & (me_c < n_ctx - 1))
        def _():
            for copy in pass_copies(source):
                copy.wait_recv()
                copy.start()

    scale = HEAD_SIZE ** -0.5 * math.log2(math.e)
    load_q.wait()

    causal = jnp.where(
        lax.broadcasted_iota(jnp.int32, (half, half), 1)
        <= lax.broadcasted_iota(jnp.int32, (half, half), 0),
        0.0, NEG,
    )
    causal = jnp.concatenate([causal] * per_kv, axis=0)

    def stacked(k, top):
        rows = slice(top * half, (top + 1) * half)
        return jnp.concatenate(
            [q_v[rows, h * HEAD_SIZE:(h + 1) * HEAD_SIZE] for h in range(k * per_kv, (k + 1) * per_kv)], axis=0
        )

    units = [(k, top) for top in (0, 1) for k in range(kv_heads)]
    for number, (k, top) in enumerate(units):
        rows = slice(top * half, (top + 1) * half)
        query = stacked(k, top)
        s = dot(query, k_v[rows, key_lanes(k)], ((1,), (1,))) * scale + causal
        best = jnp.max(s, axis=1, keepdims=True)
        if top:
            s0 = dot(query, k_v[0:half, key_lanes(k)], ((1,), (1,))) * scale
            best = jnp.max(jnp.maximum(s, s0), axis=1, keepdims=True)
        value = dot(jnp.exp2(s - best).astype(jnp.bfloat16), v_v[rows, val_wide(k)])
        if top:
            value = value + dot(jnp.exp2(s0 - best).astype(jnp.bfloat16), v_v[0:half, val_wide(k)])
        acc_s[k, top] = value
        max_s[k, top] = jnp.broadcast_to(best, max_s.shape[2:])

        if number == 0:
            for source in reversed(range(1, n_ctx - 1)):
                forward_pass(source)

        @pl.when((me_c > 0) & (me_c < n_ctx - 1))
        def _():
            for i in [number] if number < kv_heads else [2 * number - kv_heads, 2 * number - kv_heads + 1]:
                anchor_copy(i, False).wait_recv()
                anchor_copy(i, False).start()

        if number == kv_heads - 1 and n_ctx > 1:
            forward_pass(0)

    def await_remote(values):
        @pl.when((me_c == n_ctx - 1) & (me_c > 0))
        def _():
            for source in range(n_ctx - 1):
                copies = pass_copies(source)
                for copy in copies[1:] if values else copies[:1]:
                    copy.wait_recv()
            for i in range(kv_heads, pieces) if values else range(kv_heads):
                anchor_copy(i, False).wait_recv()

    await_remote(0)
    place = lax.broadcasted_iota(jnp.int32, (1, rem_rows), 1)
    seen_anchor = (place < jnp.minimum(len_ref[0], ANCHOR)) & (me_c > 0)
    seen_pass = (place >= ANCHOR) & (place - ANCHOR < me_c * retained)
    bias = jnp.where(seen_anchor | seen_pass, 0.0, NEG)

    def weigh(top):
        for k in range(kv_heads):
            s = dot(stacked(k, top), rem_k[:, key_lanes(k)], ((1,), (1,))) * scale + bias
            before = max_s[k, top]
            best = jnp.maximum(before, jnp.max(s, axis=1, keepdims=True))
            wide = jnp.concatenate([best] * (rem_rows // HEAD_SIZE), axis=1)
            p_s[k, top] = jnp.exp2(s - wide).astype(jnp.bfloat16)
            fade = jnp.exp2(before - best)
            acc_s[k, top] = acc_s[k, top] * jnp.concatenate([fade, fade], axis=1)

    def attend(top):
        rows = slice(top * half, (top + 1) * half)
        for k in range(kv_heads):
            value = acc_s[k, top] + dot(p_s[k, top], rem_v[:, val_wide(k)])
            value = (value[:, :HEAD_SIZE] / value[:, HEAD_SIZE:]).astype(jnp.bfloat16)
            for g in range(per_kv):
                h = k * per_kv + g
                att[rows, h * HEAD_SIZE:(h + 1) * HEAD_SIZE] = value[g * half:(g + 1) * half]

    def red_copy(r, c, top):
        rows = pl.ds(top * half, half)
        return pltpu.make_async_remote_copy(
            src_ref=outgoing.at[r - 1, c, rows, :], dst_ref=incoming.at[r - 1, c, rows, :],
            send_sem=red_send.at[r - 1, c, top], recv_sem=red_recv.at[r - 1, c, top],
            device_id={"head": flip(me_h, low_bit(r))}, device_id_type=MESH,
        )

    def product(r, c, rows):
        return dot(att[rows, :], w_v[r, :, c * chunk:(c + 1) * chunk])

    def with_received(total, r, c, top, first, last):
        bit = first
        while bit < last:
            red_copy(r + bit, c, top).wait_recv()
            total = total + incoming[r + bit - 1, c, top * half:(top + 1) * half, :].astype(jnp.float32)
            bit *= 2
        return total

    def send(total, r, c, top):
        outgoing[r - 1, c, top * half:(top + 1) * half, :] = total.astype(jnp.bfloat16)
        red_copy(r, c, top).start()

    middle = n_head // 2
    for r in range(middle, n_head):
        w_loads[r].wait()
    for top in (0, 1):
        rows = slice(top * half, (top + 1) * half)
        weigh(top)
        if top == 0:
            await_remote(1)
        attend(top)
        late = []
        for c in range(chunks):
            for r in reversed(range(middle, n_head)):
                value = product(r, c, rows)
                if r % 2:
                    send(value, r, c, top)
                else:
                    late.append((value, r, c))
            while len(late) > LAG:
                value, r, d = late.pop(0)
                send(with_received(value, r, d, top, 1, low_bit(r)), r, d, top)
        for value, r, d in late:
            send(with_received(value, r, d, top, 1, low_bit(r)), r, d, top)

    for r in range(middle):
        w_loads[r].wait()
    for r in reversed(range(1, middle)):
        for c in range(chunks):
            value = product(r, c, slice(0, tok))
            for top in (0, 1):
                send(with_received(value[top * half:(top + 1) * half], r, c, top, 1, low_bit(r)), r, c, top)
    for c in range(chunks):
        part[c] = product(0, c, slice(0, tok))
    for c in range(chunks):
        for top in (0, 1):
            rows = slice(top * half, (top + 1) * half)
            part[c, rows, :] = with_received(part[c, rows, :], 0, c, top, 1, middle)
    for top in (0, 1):
        rows = slice(top * half, (top + 1) * half)
        for c in range(chunks):
            total = with_received(part[c, rows, :], 0, c, top, middle, n_head)
            o_ref[rows, c * chunk:(c + 1) * chunk] = total.astype(jnp.bfloat16)

    for r in range(1, n_head):
        for c in range(chunks):
            for top in (0, 1):
                red_copy(r, c, top).wait_send()
    @pl.when(me_c < n_ctx - 1)
    def _():
        for i in range(pieces):
            anchor_copy(i, True).wait_send()
    for source in range(n_ctx - 1):
        @pl.when((me_c >= source) & (me_c < n_ctx - 1))
        def _():
            for copy in pass_copies(source):
                copy.wait_send()


def local(n_ctx, n_head, queries, rotated_key_rows, value_state_rows, retained_positions, anchor_length, out_proj):
    tok, q_width = queries.shape
    kv_width = rotated_key_rows.shape[1]
    retained = retained_positions.shape[1]
    rem_rows = pl.cdiv(ANCHOR + n_ctx * retained, HEAD_SIZE) * HEAD_SIZE
    slab = out_proj.shape[1] // n_head
    chunk = math.gcd(slab, 256)
    chunks = slab // chunk
    dma = pltpu.SemaphoreType.DMA
    held = pl.BlockSpec(memory_space=pltpu.HBM)
    per_kv = q_width // kv_width
    kv_heads = kv_width // HEAD_SIZE
    stack = per_kv * tok // 2
    operands = [
        pltpu.with_memory_space_constraint(array, pltpu.HBM)
        for array in (retained_positions, queries, rotated_key_rows, value_state_rows, out_proj)
    ]
    return pl.pallas_call(
        functools.partial(kernel, n_ctx, n_head),
        out_shape=jax.ShapeDtypeStruct((tok, slab), jnp.bfloat16),
        in_specs=[pl.BlockSpec(memory_space=pltpu.SMEM), held, held, held, held, held],
        out_specs=pl.BlockSpec(memory_space=pltpu.VMEM),
        scratch_shapes=[
            pltpu.VMEM((1, retained), jnp.int32),
            pltpu.VMEM((tok, q_width), jnp.bfloat16),
            pltpu.VMEM((tok, kv_width), jnp.bfloat16),
            pltpu.VMEM((tok, 2 * kv_width), jnp.bfloat16),
            pltpu.VMEM((rem_rows, kv_width), jnp.bfloat16),
            pltpu.VMEM((rem_rows, 2 * kv_width), jnp.bfloat16),
            pltpu.VMEM((n_head, q_width, slab), jnp.bfloat16),
            pltpu.VMEM((kv_heads, 2, stack, 2 * HEAD_SIZE), jnp.float32),
            pltpu.VMEM((kv_heads, 2, stack, HEAD_SIZE), jnp.float32),
            pltpu.VMEM((kv_heads, 2, stack, rem_rows), jnp.bfloat16),
            pltpu.VMEM((tok, q_width), jnp.bfloat16),
            pltpu.VMEM((chunks, tok, chunk), jnp.float32),
            pltpu.VMEM((n_head - 1, chunks, tok, chunk), jnp.bfloat16),
            pltpu.VMEM((n_head - 1, chunks, tok, chunk), jnp.bfloat16),
            dma((3 + kv_heads,)),
            dma((n_head,)),
            dma((n_ctx, 1 + kv_heads)),
            dma((n_ctx, 1 + kv_heads)),
            dma((3 * kv_heads,)),
            dma((3 * kv_heads,)),
            dma((n_head - 1, chunks, 2)),
            dma((n_head - 1, chunks, 2)),
        ],
        compiler_params=pltpu.CompilerParams(
            collective_id=0, has_side_effects=True, vmem_limit_bytes=48 * 1024 * 1024
        ),
    )(anchor_length, *operands)


def solution(mesh):
    placed = (
        P(("groups", "ctx"), "head"),
        P(("groups", "ctx"), "head"),
        P(("groups", "ctx"), "head"),
        P(("groups", "ctx"), None),
        P("groups"),
        P("head", None),
    )
    return jax.shard_map(
        functools.partial(local, mesh.shape["ctx"], mesh.shape["head"]),
        mesh=mesh, in_specs=placed, out_specs=P(("groups", "ctx"), "head"), check_vma=False,
    )
```

```python
import functools
import math

import jax
import jax.numpy as jnp
from jax import lax
from jax.experimental import pallas as pl
from jax.experimental.pallas import tpu as pltpu
from jax.sharding import PartitionSpec as P

HEAD_SIZE = 128
ANCHOR = 128
MESH = pl.DeviceIdType.MESH
NEG = -1e30
LAG = 1


def flip(index, mask):
    bit = 1
    while bit <= mask:
        if mask & bit:
            index = index + bit * (1 - 2 * ((index // bit) % 2))
        bit *= 2
    return index


def low_bit(r):
    return r & -r


def dot(a, b, dims=((1,), (0,))):
    return lax.dot_general(a, b, (dims, ((), ())), preferred_element_type=jnp.float32)


def kernel(
    n_ctx, n_head, len_ref, pos_hbm, q_hbm, k_hbm, v_hbm, w_hbm, o_ref,
    pos_v, q_v, k_v, v_v, rem_k, rem_v, w_v, acc_s, max_s, p_s, att, part, outgoing, incoming,
    load_sem, w_sem, pass_send, pass_recv, anc_send, anc_recv, red_send, red_recv,
):
    me_c = lax.axis_index("ctx")
    me_h = lax.axis_index("head")
    tok, q_width = q_v.shape
    kv_width = k_v.shape[1]
    kv_heads = kv_width // HEAD_SIZE
    per_kv = q_width // kv_width
    retained = pos_v.shape[1]
    rem_rows = rem_k.shape[0]
    chunks, _, chunk = part.shape
    slab = chunks * chunk
    half = tok // 2
    pieces = 2 * kv_heads

    def key_lanes(k):
        return pl.ds(k * HEAD_SIZE, HEAD_SIZE)

    def val_lanes(k):
        return pl.ds(2 * k * HEAD_SIZE, HEAD_SIZE)

    def val_wide(k):
        return pl.ds(2 * k * HEAD_SIZE, 2 * HEAD_SIZE)

    loads = [pltpu.make_async_copy(k_hbm, k_v, load_sem.at[0])]
    loads += [
        pltpu.make_async_copy(v_hbm.at[:, key_lanes(k)], v_v.at[:, val_lanes(k)], load_sem.at[3 + k])
        for k in range(kv_heads)
    ]
    loads.append(pltpu.make_async_copy(pos_hbm, pos_v, load_sem.at[1]))
    load_q = pltpu.make_async_copy(q_hbm, q_v, load_sem.at[2])
    for copy in loads:
        copy.start()
    load_q.start()

    rem_k[...] = jnp.zeros_like(rem_k)
    for k in range(kv_heads):
        ones = slice((2 * k + 1) * HEAD_SIZE, (2 * k + 2) * HEAD_SIZE)
        v_v[:, ones] = jnp.ones((tok, HEAD_SIZE), jnp.bfloat16)
        rem_v[:, ones] = jnp.ones((rem_rows, HEAD_SIZE), jnp.bfloat16)
        rem_v[:, val_lanes(k)] = jnp.zeros((rem_rows, HEAD_SIZE), jnp.bfloat16)

    barrier = pltpu.get_barrier_semaphore()
    @pl.when(me_c > 0)
    def _():
        before = lax.rem(me_c + n_ctx - 1, n_ctx)
        pl.semaphore_signal(barrier, inc=1, device_id={"ctx": before}, device_id_type=MESH)
    bit, steps = 1, 0
    while bit < n_head:
        pl.semaphore_signal(barrier, inc=1, device_id={"head": flip(me_h, bit)}, device_id_type=MESH)
        bit, steps = 2 * bit, steps + 1

    w_loads = {}
    for r in reversed(range(n_head)):
        columns = pl.ds(pl.multiple_of(flip(me_h, r) * slab, slab), slab)
        w_loads[r] = pltpu.make_async_copy(w_hbm.at[:, columns], w_v.at[r], w_sem.at[r])
        w_loads[r].start()

    def pass_copies(source):
        rows = pl.ds(pl.multiple_of(ANCHOR + source * retained, retained), retained)
        refs = [rem_k.at[rows, :]] + [rem_v.at[rows, val_lanes(k)] for k in range(kv_heads)]
        return [
            pltpu.make_async_remote_copy(
                src_ref=ref, dst_ref=ref,
                send_sem=pass_send.at[source, i], recv_sem=pass_recv.at[source, i],
                device_id={"ctx": lax.rem(me_c + 1, n_ctx)}, device_id_type=MESH,
            )
            for i, ref in enumerate(refs)
        ]

    def anchor_copy(i, origin):
        rows = pl.ds(0, ANCHOR)
        if i < kv_heads:
            source, target, lanes = k_v, rem_k, key_lanes(i)
        else:
            source, target, lanes = v_v, rem_v, val_lanes(i - kv_heads)
        return pltpu.make_async_remote_copy(
            src_ref=(source if origin else target).at[rows, lanes], dst_ref=target.at[rows, lanes],
            send_sem=anc_send.at[i], recv_sem=anc_recv.at[i],
            device_id={"ctx": lax.rem(me_c + 1, n_ctx)}, device_id_type=MESH,
        )

    for copy in loads:
        copy.wait()
    @pl.when(me_c < n_ctx - 1)
    def _():
        pl.semaphore_wait(barrier, steps + 1)

    @pl.when(me_c == n_ctx - 1)
    def _():
        pl.semaphore_wait(barrier, steps)

    def start_anchor(first, last):
        if n_ctx > 1:
            @pl.when(me_c == 0)
            def _():
                for i in range(first, last):
                    anchor_copy(i, True).start()

    start_anchor(0, kv_heads)
    picked = lax.broadcasted_iota(jnp.int32, (tok, retained), 0) == pos_v[...]
    picked = picked.astype(jnp.bfloat16)
    mine = pl.ds(pl.multiple_of(ANCHOR + me_c * retained, retained), retained)
    rem_k[mine, :] = dot(picked, k_v[...], ((0,), (0,))).astype(jnp.bfloat16)
    for k in range(kv_heads):
        rem_v[mine, val_lanes(k)] = dot(picked, v_v[:, val_lanes(k)], ((0,), (0,))).astype(jnp.bfloat16)
    @pl.when(me_c < n_ctx - 1)
    def _():
        for copy in pass_copies(me_c):
            copy.start()

    start_anchor(kv_heads, pieces)

    def forward_pass(source):
        @pl.when((me_c > source) & (me_c < n_ctx - 1))
        def _():
            for copy in pass_copies(source):
                copy.wait_recv()
                copy.start()

    scale = HEAD_SIZE ** -0.5 * math.log2(math.e)
    load_q.wait()

    causal = jnp.where(
        lax.broadcasted_iota(jnp.int32, (half, half), 1)
        <= lax.broadcasted_iota(jnp.int32, (half, half), 0),
        0.0, NEG,
    )
    causal = jnp.concatenate([causal] * per_kv, axis=0)

    def stacked(k, top):
        rows = slice(top * half, (top + 1) * half)
        return jnp.concatenate(
            [q_v[rows, h * HEAD_SIZE:(h + 1) * HEAD_SIZE] for h in range(k * per_kv, (k + 1) * per_kv)], axis=0
        )

    units = [(k, top) for top in (0, 1) for k in range(kv_heads)]
    for number, (k, top) in enumerate(units):
        rows = slice(top * half, (top + 1) * half)
        query = stacked(k, top)
        s = dot(query, k_v[rows, key_lanes(k)], ((1,), (1,))) * scale + causal
        best = jnp.max(s, axis=1, keepdims=True)
        if top:
            s0 = dot(query, k_v[0:half, key_lanes(k)], ((1,), (1,))) * scale
            best = jnp.max(jnp.maximum(s, s0), axis=1, keepdims=True)
        value = dot(jnp.exp2(s - best).astype(jnp.bfloat16), v_v[rows, val_wide(k)])
        if top:
            value = value + dot(jnp.exp2(s0 - best).astype(jnp.bfloat16), v_v[0:half, val_wide(k)])
        acc_s[k, top] = value
        max_s[k, top] = jnp.broadcast_to(best, max_s.shape[2:])

        if number == 0:
            for source in reversed(range(1, n_ctx - 1)):
                forward_pass(source)

        @pl.when((me_c > 0) & (me_c < n_ctx - 1))
        def _():
            anchor_copy(number, False).wait_recv()
            anchor_copy(number, False).start()

        if number == kv_heads - 1 and n_ctx > 1:
            forward_pass(0)

    def await_remote(values):
        @pl.when((me_c == n_ctx - 1) & (me_c > 0))
        def _():
            for source in range(n_ctx - 1):
                copies = pass_copies(source)
                for copy in copies[1:] if values else copies[:1]:
                    copy.wait_recv()
            for k in range(kv_heads):
                anchor_copy(k + values * kv_heads, False).wait_recv()

    await_remote(0)
    place = lax.broadcasted_iota(jnp.int32, (1, rem_rows), 1)
    seen_anchor = (place < jnp.minimum(len_ref[0], ANCHOR)) & (me_c > 0)
    seen_pass = (place >= ANCHOR) & (place - ANCHOR < me_c * retained)
    bias = jnp.where(seen_anchor | seen_pass, 0.0, NEG)

    def weigh(top):
        for k in range(kv_heads):
            s = dot(stacked(k, top), rem_k[:, key_lanes(k)], ((1,), (1,))) * scale + bias
            before = max_s[k, top]
            best = jnp.maximum(before, jnp.max(s, axis=1, keepdims=True))
            wide = jnp.concatenate([best] * (rem_rows // HEAD_SIZE), axis=1)
            p_s[k, top] = jnp.exp2(s - wide).astype(jnp.bfloat16)
            fade = jnp.exp2(before - best)
            acc_s[k, top] = acc_s[k, top] * jnp.concatenate([fade, fade], axis=1)

    def attend(top):
        rows = slice(top * half, (top + 1) * half)
        for k in range(kv_heads):
            value = acc_s[k, top] + dot(p_s[k, top], rem_v[:, val_wide(k)])
            value = (value[:, :HEAD_SIZE] / value[:, HEAD_SIZE:]).astype(jnp.bfloat16)
            for g in range(per_kv):
                h = k * per_kv + g
                att[rows, h * HEAD_SIZE:(h + 1) * HEAD_SIZE] = value[g * half:(g + 1) * half]

    def red_copy(r, c, top):
        rows = pl.ds(top * half, half)
        return pltpu.make_async_remote_copy(
            src_ref=outgoing.at[r - 1, c, rows, :], dst_ref=incoming.at[r - 1, c, rows, :],
            send_sem=red_send.at[r - 1, c, top], recv_sem=red_recv.at[r - 1, c, top],
            device_id={"head": flip(me_h, low_bit(r))}, device_id_type=MESH,
        )

    def product(r, c, rows):
        return dot(att[rows, :], w_v[r, :, c * chunk:(c + 1) * chunk])

    def with_received(total, r, c, top, first, last):
        bit = first
        while bit < last:
            red_copy(r + bit, c, top).wait_recv()
            total = total + incoming[r + bit - 1, c, top * half:(top + 1) * half, :].astype(jnp.float32)
            bit *= 2
        return total

    def send(total, r, c, top):
        outgoing[r - 1, c, top * half:(top + 1) * half, :] = total.astype(jnp.bfloat16)
        red_copy(r, c, top).start()

    middle = n_head // 2
    for r in range(middle, n_head):
        w_loads[r].wait()
    for top in (0, 1):
        rows = slice(top * half, (top + 1) * half)
        weigh(top)
        if top == 0:
            await_remote(1)
        attend(top)
        late = []
        for c in range(chunks):
            for r in reversed(range(middle, n_head)):
                value = product(r, c, rows)
                if r % 2:
                    send(value, r, c, top)
                else:
                    late.append((value, r, c))
            while len(late) > LAG:
                value, r, d = late.pop(0)
                send(with_received(value, r, d, top, 1, low_bit(r)), r, d, top)
        for value, r, d in late:
            send(with_received(value, r, d, top, 1, low_bit(r)), r, d, top)

    for r in range(middle):
        w_loads[r].wait()
    for r in reversed(range(1, middle)):
        for c in range(chunks):
            value = product(r, c, slice(0, tok))
            for top in (0, 1):
                send(with_received(value[top * half:(top + 1) * half], r, c, top, 1, low_bit(r)), r, c, top)
    for c in range(chunks):
        part[c] = product(0, c, slice(0, tok))
    for c in range(chunks):
        for top in (0, 1):
            rows = slice(top * half, (top + 1) * half)
            part[c, rows, :] = with_received(part[c, rows, :], 0, c, top, 1, middle)
    for top in (0, 1):
        rows = slice(top * half, (top + 1) * half)
        for c in range(chunks):
            total = with_received(part[c, rows, :], 0, c, top, middle, n_head)
            o_ref[rows, c * chunk:(c + 1) * chunk] = total.astype(jnp.bfloat16)

    for r in range(1, n_head):
        for c in range(chunks):
            for top in (0, 1):
                red_copy(r, c, top).wait_send()
    @pl.when(me_c < n_ctx - 1)
    def _():
        for i in range(pieces):
            anchor_copy(i, True).wait_send()
    for source in range(n_ctx - 1):
        @pl.when((me_c >= source) & (me_c < n_ctx - 1))
        def _():
            for copy in pass_copies(source):
                copy.wait_send()


def local(n_ctx, n_head, queries, rotated_key_rows, value_state_rows, retained_positions, anchor_length, out_proj):
    tok, q_width = queries.shape
    kv_width = rotated_key_rows.shape[1]
    retained = retained_positions.shape[1]
    rem_rows = pl.cdiv(ANCHOR + n_ctx * retained, HEAD_SIZE) * HEAD_SIZE
    slab = out_proj.shape[1] // n_head
    chunk = math.gcd(slab, 512)
    chunks = slab // chunk
    dma = pltpu.SemaphoreType.DMA
    held = pl.BlockSpec(memory_space=pltpu.HBM)
    per_kv = q_width // kv_width
    kv_heads = kv_width // HEAD_SIZE
    stack = per_kv * tok // 2
    operands = [
        pltpu.with_memory_space_constraint(array, pltpu.HBM)
        for array in (retained_positions, queries, rotated_key_rows, value_state_rows, out_proj)
    ]
    return pl.pallas_call(
        functools.partial(kernel, n_ctx, n_head),
        out_shape=jax.ShapeDtypeStruct((tok, slab), jnp.bfloat16),
        in_specs=[pl.BlockSpec(memory_space=pltpu.SMEM), held, held, held, held, held],
        out_specs=pl.BlockSpec(memory_space=pltpu.VMEM),
        scratch_shapes=[
            pltpu.VMEM((1, retained), jnp.int32),
            pltpu.VMEM((tok, q_width), jnp.bfloat16),
            pltpu.VMEM((tok, kv_width), jnp.bfloat16),
            pltpu.VMEM((tok, 2 * kv_width), jnp.bfloat16),
            pltpu.VMEM((rem_rows, kv_width), jnp.bfloat16),
            pltpu.VMEM((rem_rows, 2 * kv_width), jnp.bfloat16),
            pltpu.VMEM((n_head, q_width, slab), jnp.bfloat16),
            pltpu.VMEM((kv_heads, 2, stack, 2 * HEAD_SIZE), jnp.float32),
            pltpu.VMEM((kv_heads, 2, stack, HEAD_SIZE), jnp.float32),
            pltpu.VMEM((kv_heads, 2, stack, rem_rows), jnp.bfloat16),
            pltpu.VMEM((tok, q_width), jnp.bfloat16),
            pltpu.VMEM((chunks, tok, chunk), jnp.float32),
            pltpu.VMEM((n_head - 1, chunks, tok, chunk), jnp.bfloat16),
            pltpu.VMEM((n_head - 1, chunks, tok, chunk), jnp.bfloat16),
            dma((3 + kv_heads,)),
            dma((n_head,)),
            dma((n_ctx, 1 + kv_heads)),
            dma((n_ctx, 1 + kv_heads)),
            dma((2 * kv_heads,)),
            dma((2 * kv_heads,)),
            dma((n_head - 1, chunks, 2)),
            dma((n_head - 1, chunks, 2)),
        ],
        compiler_params=pltpu.CompilerParams(
            collective_id=0, has_side_effects=True, vmem_limit_bytes=48 * 1024 * 1024
        ),
    )(anchor_length, *operands)


def solution(mesh):
    placed = (
        P(("groups", "ctx"), "head"),
        P(("groups", "ctx"), "head"),
        P(("groups", "ctx"), "head"),
        P(("groups", "ctx"), None),
        P("groups"),
        P("head", None),
    )
    return jax.shard_map(
        functools.partial(local, mesh.shape["ctx"], mesh.shape["head"]),
        mesh=mesh, in_specs=placed, out_specs=P(("groups", "ctx"), "head"), check_vma=False,
    )
```
